512 devices in a mesh: lon: 64 (over y, z_lo, core), lat: 8 (over x, z_hi).
Axes of the slice: x: 4, y: 4, z: 16 (z_hi: 2, z_lo: 8; z = z_hi * 8 + z_lo), core: 2. Of those that a mesh axis runs over, the one named last changes fastest.
Arguments:
- latent: bfloat16 [2, 48, 1536, 192], P(None, 'lat', 'lon'), may hold values from -6 to 6
- out_grad: bfloat16 [2, 48, 1536, 192], P(None, 'lat', 'lon'), may hold values from -6 to 6
- norm_gain: float32 [192], replicated, may hold values from 0.1 to 1.9
- norm_shift: float32 [192], replicated, may hold values from -3 to 3
- qkv_weight: bfloat16 [192, 576], replicated, may hold values from -0.4375 to 0.4375
- query_bias: float32 [192], replicated, may hold values from -3 to 3
- proj_weight: bfloat16 [192, 192], replicated, may hold values from -0.4375 to 0.4375
- bias_table: float32 [8, 1, 6, 3312], P('lat'), may hold values from -3 to 3
- band_rows: int32 [8], P('lat'), may hold values from 0 to 7, as said below
Outputs:
- latent_grad: bfloat16 [2, 48, 1536, 192], P(None, 'lat', 'lon')
- table_grad: float32 [8, 1, 6, 3312], P('lat')
The draws below stay inside these ranges and needn't reach their ends.
Inputs may be any that keep to these rules, and one draw needn't show every extreme that they name: `band_rows`: in each aligned block of 1 entries, starting at 1 * k, the entries are a permutation of 1 * k to 1 * k + 1 - 1.
All inputs are finite; a program needn't handle non-finite values.
Results may differ from the reference program's by a relative error of at most 0.0099.
Values may be sent and summed in bfloat16 or wider, within the bound.
A program may use at most 128 MiB of HBM per device.

```python
import jax
import jax.numpy as jnp
from jax import lax

D = 192
HEADS = 6
WPL = 2
WLAT = 6
WLON = 12
REL = 3312
PL = 2
LAT_DEV = 6
LATWIN = 8
LAT = 48
LON = 1536


def draw_band_rows(key, part):
    key = jax.random.fold_in(key, 7)
    per_block = LAT_DEV // WLAT
    blocks = LATWIN // per_block
    scores = jax.random.randint(key, (blocks, per_block), 0, 1000) * per_block + jnp.arange(per_block)[None, :]
    ranking = jnp.argsort(scores, axis=1)
    return (ranking + per_block * jnp.arange(blocks)[:, None]).reshape(-1).astype(jnp.int32)


def level_of(rng, extent, split, low, largest):
    level, own = 1.0, jax.random.fold_in(rng, 6)
    for axis_at, parts in split:
        draws = jnp.exp(jax.random.uniform(jax.random.fold_in(own, axis_at), (parts,), jnp.float32, low / len(split), largest / len(split)))
        level = level * jnp.repeat(draws, extent[axis_at] // parts).reshape([-1 if axis == axis_at else 1 for axis in range(len(extent))])
    return level


def noise(stream_key, shape, scale, most, pieces=(), held_as=jnp.bfloat16):
    entries = jax.random.normal(stream_key, shape, jnp.float32) * scale
    if len(pieces) > 0:
        entries = level_of(stream_key, shape, pieces, -0.22, 0.18) * entries
    return jnp.clip(entries, min=-most, max=most).astype(held_as)


def setup_inputs(seed: int = 0) -> dict:
    key_of = jax.random.split(jax.random.key(seed), 10)
    return {
        "latent": noise(key_of[0], (PL, LAT, LON, D), 1.0, 6.0, ((1, 8), (2, 64))),
        "out_grad": noise(key_of[1], (PL, LAT, LON, D), 1.0, 6.0, ((1, 8), (2, 64))),
        "norm_gain": jnp.clip(1.0 + 0.18 * jax.random.normal(key_of[2], (D,), jnp.float32), 0.1, 1.9),
        "norm_shift": noise(key_of[3], (D,), 0.5, 3.0, (), jnp.float32),
        "qkv_weight": noise(key_of[4], (D, 3 * D), D ** -0.5, 0.4375),
        "query_bias": noise(key_of[5], (D,), 0.5, 3.0, (), jnp.float32),
        "proj_weight": noise(key_of[6], (D, D), D ** -0.5, 0.4375),
        "bias_table": noise(key_of[7], (LATWIN, PL // WPL, HEADS, REL), 0.5, 3.0, ((0, 8),), jnp.float32),
        "band_rows": draw_band_rows(jax.random.fold_in(key_of[9], 71), 0),
    }


EPSILON = 1e-05
HIGHEST_PRECISION = lax.Precision.HIGHEST

def widen(narrow):
    return lax.optimization_barrier(narrow).astype(jnp.float32)

def pair_index():
    tokens_at = jnp.arange(WPL * WLAT * WLON, dtype=jnp.int32)
    level_pos = tokens_at // (WLAT * WLON)
    row_pos = tokens_at // WLON % WLAT
    column_pos = tokens_at % WLON
    offset_span = 2 * WLON - 1
    return column_pos[:, None] - column_pos[None, :] + WLON - 1 + offset_span * (row_pos[:, None] * WLAT + row_pos[None, :]) + offset_span * WLAT * WLAT * (level_pos[:, None] * WPL + level_pos[None, :])

def shift_onehot():
    columns = jnp.arange(WLON, dtype=jnp.int32)
    offsets = jnp.arange(2 * WLON - 1, dtype=jnp.int32)
    return (columns[None, :, None] - columns[None, None, :] + WLON - 1 == offsets[:, None, None]).astype(jnp.float32)

def attention_grads(tokens, incoming, bias_win, allowed, norm_gain, norm_shift, qkv_weight, query_bias, proj_weight):
    features = tokens.shape[-1]
    head_size = features // HEADS
    factor = head_size ** (-0.5)
    head_shape = tokens.shape[:-1] + (HEADS, head_size)
    values = tokens.astype(jnp.float32)
    center = lax.optimization_barrier(jnp.mean(values, -1, keepdims=True))
    spread = lax.optimization_barrier(jnp.mean(jnp.square(values - center), -1, keepdims=True))
    inverse = lax.rsqrt(spread + EPSILON)
    normed = (values - center) * inverse
    hidden = (normed * norm_gain + norm_shift).astype(jnp.bfloat16)
    projected = jnp.dot(hidden, qkv_weight, preferred_element_type=jnp.float32)
    queries = (projected[..., :features] + query_bias).astype(jnp.bfloat16).reshape(head_shape)
    keys_low = projected[..., features:2 * features].astype(jnp.bfloat16).reshape(head_shape)
    vals_low = projected[..., 2 * features:].astype(jnp.bfloat16).reshape(head_shape)
    scores = factor * jnp.einsum('...ihe,...jhe->...hij', widen(queries), widen(keys_low)) + bias_win
    weights = jnp.where(allowed, jnp.exp(scores), 0.0)
    probabilities = weights / lax.optimization_barrier(jnp.sum(weights, -1, keepdims=True))
    upstream = jnp.dot(incoming, proj_weight.T, preferred_element_type=jnp.float32).astype(jnp.bfloat16).reshape(head_shape)
    prob_grad = jnp.einsum('...ihe,...jhe->...hij', widen(upstream), widen(vals_low))
    value_grad = jnp.einsum('...hij,...ihe->...jhe', widen(probabilities.astype(jnp.bfloat16)), widen(upstream)).astype(jnp.bfloat16)
    score_grad = probabilities * (prob_grad - lax.optimization_barrier(jnp.sum(probabilities * prob_grad, -1, keepdims=True)))
    score_low = widen(score_grad.astype(jnp.bfloat16))
    query_grad = (factor * jnp.einsum('...hij,...jhe->...ihe', score_low, widen(keys_low))).astype(jnp.bfloat16)
    key_grad = (factor * jnp.einsum('...hij,...ihe->...jhe', score_low, widen(queries))).astype(jnp.bfloat16)
    stacked = jnp.concatenate([query_grad.reshape(tokens.shape), key_grad.reshape(tokens.shape), value_grad.reshape(tokens.shape)], -1)
    hidden_grad = jnp.dot(stacked, qkv_weight.T, preferred_element_type=jnp.float32)
    normed_grad = hidden_grad * norm_gain
    branch = inverse * (normed_grad - lax.optimization_barrier(jnp.mean(normed_grad, -1, keepdims=True)) - normed * lax.optimization_barrier(jnp.mean(normed_grad * normed, -1, keepdims=True)))
    return (branch, score_grad)

def reference(latent, out_grad, norm_gain, norm_shift, qkv_weight, query_bias, proj_weight, bias_table, band_rows):
    levels, lat_rows, lon_cols, features = latent.shape
    level_wins = levels // WPL
    lat_wins = lat_rows // WLAT
    lon_wins = lon_cols // WLON
    window_size = WPL * WLAT * WLON
    offsets = (-(WPL // 2), -(WLAT // 2), -(WLON // 2))
    rolled_latent = jnp.roll(latent, offsets, axis=(0, 1, 2))
    rolled_grad = jnp.roll(out_grad, offsets, axis=(0, 1, 2))
    level_flag = (jnp.arange(levels) >= levels - WPL // 2).astype(jnp.int32)
    lat_flag = (jnp.arange(lat_rows) >= lat_rows - WLAT // 2).astype(jnp.int32)
    groups = level_flag[:, None] * 2 + lat_flag[None, :]
    groups = groups.reshape(level_wins, WPL, lat_wins, WLAT).transpose(0, 2, 1, 3)
    groups = jnp.broadcast_to(groups[..., None], (level_wins, lat_wins, WPL, WLAT, WLON)).reshape(level_wins, lat_wins, window_size)
    allowed = (groups[:, :, :, None] == groups[:, :, None, :])[:, :, None, :, :]
    chosen = jnp.transpose(bias_table[band_rows], (1, 0, 2, 3))
    attn_bias = chosen[..., pair_index()]
    onehot = shift_onehot()

    def to_windows(block):
        return block.reshape(level_wins, WPL, lat_wins, WLAT, WLON, features).transpose(0, 2, 1, 3, 4, 5).reshape(level_wins, lat_wins, window_size, features)

    def window_step(table_acc, column):
        first_col = column * WLON
        block_latent = lax.dynamic_slice_in_dim(rolled_latent, first_col, WLON, 2)
        block_grad = lax.dynamic_slice_in_dim(rolled_grad, first_col, WLON, 2)
        branch, score_grad = attention_grads(to_windows(block_latent), to_windows(block_grad), attn_bias, allowed, norm_gain, norm_shift, qkv_weight, query_bias, proj_weight)
        unfolded = score_grad.reshape(level_wins, lat_wins, HEADS, WPL, WLAT, WLON, WPL, WLAT, WLON)
        folded = jnp.einsum('xlhpaoqbr,dor->xlhpqabd', unfolded, onehot, precision=HIGHEST_PRECISION)
        return (table_acc + folded.reshape(level_wins, lat_wins, HEADS, REL), branch)
    table_init = jnp.zeros((level_wins, lat_wins, HEADS, REL), jnp.float32)
    table_acc, branches = lax.scan(window_step, table_init, jnp.arange(lon_wins, dtype=jnp.int32))
    field_grad = branches.reshape(lon_wins, level_wins, lat_wins, WPL, WLAT, WLON, features)
    field_grad = field_grad.transpose(1, 3, 2, 4, 0, 5, 6).reshape(levels, lat_rows, lon_cols, features)
    restored = jnp.roll(field_grad, (WPL // 2, WLAT // 2, WLON // 2), axis=(0, 1, 2))
    latent_grad = (out_grad.astype(jnp.float32) + restored).astype(jnp.bfloat16)
    table_grad = jnp.zeros((lat_wins, level_wins, HEADS, REL), jnp.float32).at[band_rows].add(jnp.transpose(table_acc, (1, 0, 2, 3)))
    return (latent_grad, table_grad)
```

```python
import functools

import jax
import jax.numpy as jnp
import ml_dtypes
import numpy as np
from jax import lax
from jax.experimental import pallas as pl
from jax.experimental.pallas import tpu as pltpu
from jax.sharding import PartitionSpec as P

HEADS = 6
D = 192
WLAT = 6
WLON = 12
ROWS = 6
COLS = 24
REL = 3312
SPAN = 2 * WLON - 1
FLAT = SPAN * WLAT * WLAT
EPSILON = 1e-05
SCALE = 32 ** (-0.5)
TOK = ROWS * COLS
WTOK = 96
BOTH = 2 * WTOK
FWD = ((0, 176), (176, 64), (240, 64))
FWD_ROWS = 304
RET = ((0, 96), (96, 32), (128, 32))
RET_ROWS = 160
LANES = HEADS * 128
WIDE = 896
MASKED = -1e30
MESH = pl.DeviceIdType.MESH


def constants():
    def token(row, col):
        return row * COLS + col

    def wrow(rolled_row, rolled_col):
        return (rolled_col // WLON) * WTOK + (rolled_col % WLON) * 8 + rolled_row

    lat = [(r, c) for r in range(3) for c in range(6, COLS)]
    diag = [(r, c) for r in range(3) for c in range(6)]
    lon = [(r, c) for r in range(3, ROWS) for c in range(6)]
    groups = (
        [(token(r, c), wrow(r + 3, c - 6)) for r, c in lat],
        [(token(r, c), wrow(r + 3, c + 18)) for r, c in diag],
        [(token(r, c), wrow(r - 3, c + 18)) for r, c in lon],
    )
    own = [(token(r, c), wrow(r - 3, c - 6)) for r in range(3, ROWS) for c in range(6, COLS)]

    pack = np.zeros((FWD_ROWS, 3 * TOK), np.float32)
    take_remote = np.zeros((3 * BOTH, FWD_ROWS), np.float32)
    ret_pack = np.zeros((RET_ROWS, 3 * BOTH), np.float32)
    put_remote = np.zeros((3 * TOK, RET_ROWS), np.float32)
    for (at, _), (back, _), group in zip(FWD, RET, groups):
        n = len(group)
        for k, (t, w) in enumerate(group):
            for part in range(3):
                pack[at + part * n + k, part * TOK + t] = 1
                take_remote[part * BOTH + w, at + part * n + k] = 1
            ret_pack[back + k, w] = 1
            put_remote[t, back + k] = 1
            high = k >= n // 2
            slot = back + n + k % (n // 2)
            ret_pack[slot, (2 if high else 1) * BOTH + w] = 1
            put_remote[(2 if high else 1) * TOK + t, slot] = 1
    take_own = np.zeros((3 * BOTH, 3 * TOK), np.float32)
    put_own = np.zeros((TOK, BOTH), np.float32)
    for t, w in own:
        put_own[t, w] = 1
        for part in range(3):
            take_own[part * BOTH + w, part * TOK + t] = 1
    tails = np.zeros((2, D, 128), np.float32)
    for i in range(64):
        tails[0, 128 + i, i] = 1
        tails[1, 128 + i, 64 + i] = 1
    spread = np.zeros((256, WIDE), np.float32)
    for d in range(SPAN):
        for a in range(WLAT):
            spread[8 * d + a, SPAN * WLAT * a + d] = 1
    qkv_pad = np.zeros((3 * D, LANES), np.float32)
    for part in range(3):
        for i in range(D):
            qkv_pad[part * D + i, part * 256 + i] = 1
    proj_pad = np.zeros((D, 256), np.float32)
    for i in range(D):
        proj_pad[i, i if i < 128 else 64 + i] = 1
    head_mask = np.zeros((16, 256), np.float32)
    for h in range(HEADS):
        head_mask[h, h * 32 : (h + 1) * 32] = 1
    matrices = (
        pack,
        tails.reshape(2 * D, 128),
        take_own,
        take_remote,
        ret_pack,
        put_own,
        put_remote,
        spread,
        qkv_pad,
        proj_pad,
        head_mask,
    )
    return tuple(m.astype(ml_dtypes.bfloat16) for m in matrices)


def dot(a, b):
    return jnp.dot(a, b, preferred_element_type=jnp.float32)


def dot_nt(a, b):
    return lax.dot_general(a, b, (((1,), (1,)), ((), ())), preferred_element_type=jnp.float32)


def dot_tn(a, b):
    return lax.dot_general(a, b, (((0,), (0,)), ((), ())), preferred_element_type=jnp.float32)


def low(a):
    return a.astype(jnp.bfloat16)


def kernel(n_lon, n_lat, n_in, *refs):
    ins, refs = refs[:n_in], refs[n_in:]
    (grad_out, table_out), refs = refs[:2], refs[2:]
    held, refs = refs[:n_in], refs[n_in:]
    (
        send_buf,
        recv_buf,
        ret_send,
        ret_recv,
        x_own,
        bias,
        table_pad,
        fold_buf,
        vecs,
        w_qkv,
        w_proj,
        q_heads,
        u_heads,
        branch_buf,
        red_src,
        red_in,
        z_slots,
        all_slots,
        in_sem,
        fwd_send,
        fwd_recv,
        back_send,
        back_recv,
        red_send,
        red_recv,
        z_send,
        z_recv,
        all_send,
        all_recv,
    ) = refs
    (
        latent,
        out_grad,
        gain,
        shift,
        qkv_weight,
        query_bias,
        proj_weight,
        bias_table,
        pack,
        tails,
        take_own,
        take_remote,
        ret_pack,
        put_own,
        put_remote,
        spread,
        qkv_pad,
        proj_pad,
        head_mask,
    ) = held

    lon, lat = lax.axis_index("lon"), lax.axis_index("lat")
    lon_m, lon_p = lax.rem(lon + n_lon - 1, n_lon), lax.rem(lon + 1, n_lon)
    lat_m, lat_p = lax.rem(lat + n_lat - 1, n_lat), lax.rem(lat + 1, n_lat)

    def at(lon_at, lat_at):
        return {"lon": lon_at, "lat": lat_at}

    before = (at(lon, lat_m), at(lon_m, lat_m), at(lon_m, lat))
    behind = (at(lon, lat_p), at(lon_p, lat_p), at(lon_p, lat))
    z_me = lax.rem(lon // 2, 8)
    y_me = lon // 16
    plane_me = y_me * 2 + lax.rem(lon, 2)

    def plane_peer(step):
        rank = lax.rem(plane_me + step, 8)
        return rank, at(((rank // 2) * 8 + z_me) * 2 + lax.rem(rank, 2), lat)

    def z_peer(step):
        z = lax.rem(z_me + step, 8)
        return at((y_me * 8 + z) * 2 + lax.rem(lon, 2), lat)

    barrier = pltpu.get_barrier_semaphore()
    everyone = list(before) + list(behind)
    everyone += [z_peer(s) for s in range(1, 8)] + [plane_peer(s)[1] for s in range(1, 8)]
    for peer in everyone:
        pl.semaphore_signal(barrier, inc=1, device_id=peer, device_id_type=MESH)

    loads = [pltpu.make_async_copy(s, d, in_sem.at[i]) for i, (s, d) in enumerate(zip(ins, held))]
    order = [0, 1, 9, 8, 10, 4, 16, 6, 17, 15, 7, 2, 3, 5, 18, 11, 12, 13, 14]
    for i in order:
        loads[i].start()
    for i in (0, 1, 9, 8):
        loads[i].wait()

    sources = []
    for p in range(2):
        rows = pl.ds((1 - p) * TOK, TOK)
        mixed = dot(latent[rows, :], tails[0:D, :]) + dot(out_grad[rows, :], tails[D : 2 * D, :])
        source = jnp.concatenate([latent[rows, 0:128], out_grad[rows, 0:128], low(mixed)], 0)
        sources.append(source)
        send_buf[p] = low(dot(pack[...], source))

    pl.semaphore_wait(barrier, len(everyone))
    forward = []
    for p in range(2):
        for g, (start, size) in enumerate(FWD):
            copy = pltpu.make_async_remote_copy(
                src_ref=send_buf.at[p, pl.ds(start, size)],
                dst_ref=recv_buf.at[p, pl.ds(start, size)],
                send_sem=fwd_send.at[p, g],
                recv_sem=fwd_recv.at[p, g],
                device_id=before[g],
                device_id_type=MESH,
            )
            copy.start()
            forward.append(copy)

    for i in order:
        if i not in (0, 1, 9, 8):
            loads[i].wait()

    for p in range(2):
        x_own[p] = dot(take_own[...], sources[p])

    w_qkv[0:D, :] = low(dot(qkv_weight[...], qkv_pad[...]))
    w_qkv[D:256, :] = jnp.zeros((256 - D, LANES), jnp.bfloat16)
    w_proj[0:D, :] = low(dot(proj_weight[...], proj_pad[...]))
    w_proj[D:256, :] = jnp.zeros((256 - D, 256), jnp.bfloat16)
    vecs[...] = jnp.zeros((8, 256), jnp.float32)
    vecs[0:1, 0:D] = gain[...]
    vecs[1:2, 0:D] = shift[...]
    vecs[2:3, 0:D] = query_bias[...]
    q_heads[...] = jnp.zeros((LANES, 256), jnp.bfloat16)
    u_heads[...] = jnp.zeros((LANES, 256), jnp.bfloat16)

    lane8 = lax.broadcasted_iota(jnp.int32, (8, 128), 1)
    row8 = lax.broadcasted_iota(jnp.int32, (8, 128), 0)
    last = (lat == n_lat - 1).astype(jnp.int32)
    query_half = (lax.rem(lane8, 8) >= 3).astype(jnp.int32)
    key_half = (row8 >= 3).astype(jnp.int32)
    left_out = (row8 >= WLAT).astype(jnp.int32) + last * (query_half ^ key_half) > 0

    for p in range(2):
        table_pad[...] = jnp.zeros((8, WIDE), jnp.float32)
        if p == 0:
            table_pad[0:HEADS, :] = bias_table[:, 0:WIDE]
        else:
            table_pad[0:HEADS, 0 : REL - 2432] = bias_table[:, 2432:REL]
        entries = table_pad[...]
        for b in range(8):
            if b < WLAT:
                moved = pltpu.roll(entries, (2 * WIDE - SPAN * b - 52 * p) % WIDE, 1)
                top = low(moved)
                rest = low(moved - top.astype(jnp.float32))
                row = dot_nt(top, spread[...]) + dot_nt(rest, spread[...])
            else:
                row = jnp.zeros((8, 256), jnp.float32)
            fold_buf[0, 8 * b : 8 * b + 8, :] = row[:, 0:128]
            fold_buf[1, 8 * b : 8 * b + 8, :] = row[:, 128:256]
        for h in range(HEADS):
            near = fold_buf[0, pl.ds(h, 8, stride=8), :]
            far = fold_buf[1, pl.ds(h, 8, stride=8), :]
            for r in range(WLON):
                s = 8 * (WLON - 1 - r)
                if s:
                    block = pltpu.roll(jnp.where(lane8 >= s, near, far), 128 - s, 1)
                else:
                    block = near
                bias[p, 8 * r : 8 * r + 8, 128 * h : 128 * h + 128] = jnp.where(left_out, MASKED, block)

    gain_w, shift_w, query_w = vecs[0:1, :], vecs[1:2, :], vecs[2:3, :]
    below64 = lax.broadcasted_iota(jnp.int32, (BOTH, 128), 1) < 64
    low_lane = lax.broadcasted_iota(jnp.int32, (BOTH, 256), 1) < D
    backward = []
    flats = []
    own_parts = []

    for p in range(2):
        for g in range(3):
            forward[3 * p + g].wait_recv()
        tokens = x_own[p] + dot(take_remote[...], recv_buf[p])
        x_a, x_b, x_c = tokens[0:BOTH], tokens[BOTH : 2 * BOTH], tokens[2 * BOTH :]
        tail = jnp.where(below64, x_c, 0.0)
        center = (jnp.sum(x_a, 1, keepdims=True) + jnp.sum(tail, 1, keepdims=True)) * (1.0 / D)
        c_a = x_a - center
        c_t = jnp.where(below64, x_c - center, 0.0)
        spread_sq = (
            jnp.sum(c_a * c_a, 1, keepdims=True) + jnp.sum(c_t * c_t, 1, keepdims=True)
        ) * (1.0 / D)
        inverse = lax.rsqrt(spread_sq + EPSILON)
        normed = jnp.concatenate([c_a, c_t], 1) * inverse
        hidden = low(normed * gain_w + shift_w)
        projected = dot(hidden, w_qkv[...])
        queries = low(projected[:, 0:256] + query_w)
        keys = low(projected[:, 256:512])
        values = low(projected[:, 512:768])
        incoming = low(jnp.concatenate([x_b, x_c], 1))
        upstream = low(dot_nt(incoming, w_proj[...]))

        score_lows, prob_lows = [], []
        score_sum = None
        for w in range(2):
            span = slice(w * WTOK, (w + 1) * WTOK)
            for h in range(HEADS):
                mask = head_mask[h : h + 1, :]
                q_heads[pl.ds(h * 128, WTOK), :] = queries[span] * mask
                u_heads[pl.ds(h * 128, WTOK), :] = upstream[span] * mask
            scores = dot_nt(keys[span], q_heads[...]) * SCALE + bias[p]
            weights = jnp.exp(scores)
            probs = weights * (1.0 / jnp.sum(weights, 0, keepdims=True))
            prob_grad = dot_nt(values[span], u_heads[...])
            inner = jnp.sum(probs * prob_grad, 0, keepdims=True)
            score_grad = probs * (prob_grad - inner)
            score_sum = score_grad if score_sum is None else score_sum + score_grad
            score_low = low(score_grad)
            value_g = dot(low(probs), u_heads[...])
            key_g = dot(score_low, q_heads[...]) * SCALE
            query_all = dot_tn(score_low, keys[span])
            query_g = None
            for h in range(HEADS):
                term = query_all[h * 128 : h * 128 + WTOK] * head_mask[h : h + 1, :].astype(jnp.float32)
                query_g = term if query_g is None else query_g + term
            score_lows.append(jnp.concatenate([low(query_g * SCALE), low(key_g), low(value_g)], 1))

        for h in range(HEADS):
            near = far = None
            for r in range(WLON):
                s = 8 * (WLON - 1 - r)
                block = score_sum[8 * r : 8 * r + 8, 128 * h : 128 * h + 128]
                if s:
                    block = pltpu.roll(block, s, 1)
                    wrapped = jnp.where(lane8 < s, block, 0.0)
                    block = jnp.where(lane8 < s, 0.0, block)
                    far = wrapped if far is None else far + wrapped
                near = block if near is None else near + block
            fold_buf[0, 8 * h : 8 * h + 8, :] = near
            fold_buf[1, 8 * h : 8 * h + 8, :] = far
        by_row = [
            jnp.concatenate([fold_buf[part, pl.ds(b, 8, stride=8), :] for part in range(2)], 1)
            for b in range(WLAT)
        ]
        lines = dot(low(jnp.concatenate(by_row, 0)), spread[...])
        flat = None
        for b in range(WLAT):
            line = lines[8 * b : 8 * b + 8]
            if b or p:
                line = pltpu.roll(line, SPAN * b + 52 * p, 1)
            flat = line if flat is None else flat + line
        flats.append(flat)

        if p == 1:
            for c in range(8):
                for half in range(2):
                    tile = 2 * c + half
                    if tile < 14:
                        part = flats[tile // 7][:, 128 * (tile % 7) : 128 * (tile % 7) + 128]
                    else:
                        part = jnp.zeros((8, 128), jnp.float32)
                    all_slots[c, 8 * half : 8 * half + 8, :] = part
                red_src[c] = low(all_slots[c])
            reduced = []
            for s in range(1, 8):
                rank, peer = plane_peer(s)
                copy = pltpu.make_async_remote_copy(
                    src_ref=red_src.at[rank],
                    dst_ref=red_in.at[s - 1],
                    send_sem=red_send.at[s - 1],
                    recv_sem=red_recv.at[s - 1],
                    device_id=peer,
                    device_id_type=MESH,
                )
                copy.start()
                reduced.append(copy)

        hidden_grad = dot_nt(jnp.concatenate(score_lows, 0), w_qkv[...])
        scaled = hidden_grad * gain_w
        mean_g = jnp.sum(scaled, 1, keepdims=True) * (1.0 / D)
        mean_gn = jnp.sum(scaled * normed, 1, keepdims=True) * (1.0 / D)
        branch = jnp.where(low_lane, inverse * (scaled - mean_g - normed * mean_gn), 0.0)
        second = branch[:, 128:256]
        stacked = jnp.concatenate([branch[:, 0:128], second, pltpu.roll(second, 64, 1)], 0)
        ret_send[p] = low(dot(ret_pack[...], low(stacked)))
        for g, (start, size) in enumerate(RET):
            copy = pltpu.make_async_remote_copy(
                src_ref=ret_send.at[p, pl.ds(start, size)],
                dst_ref=ret_recv.at[p, pl.ds(start, size)],
                send_sem=back_send.at[p, g],
                recv_sem=back_recv.at[p, g],
                device_id=behind[g],
                device_id_type=MESH,
            )
            copy.start()
            backward.append(copy)
        branch_buf[p] = low(branch)

    for copy in reduced:
        copy.wait_recv()
    total = red_src[plane_me].astype(jnp.float32)
    for s in range(7):
        total = total + red_in[s].astype(jnp.float32)
    z_slots[z_me] = low(total)
    along = []
    for s in range(1, 8):
        copy = pltpu.make_async_remote_copy(
            src_ref=z_slots.at[z_me],
            dst_ref=z_slots.at[z_me],
            send_sem=z_send.at[s - 1],
            recv_sem=z_recv.at[s - 1],
            device_id=z_peer(s),
            device_id_type=MESH,
        )
        copy.start()
        along.append(copy)

    for p in range(2):
        rows = pl.ds((1 - p) * TOK, TOK)
        own = dot(put_own[...], branch_buf[p])
        own_parts.append(
            (
                own[:, 0:128] + out_grad[rows, 0:128].astype(jnp.float32),
                own[:, 128:D] + out_grad[rows, 128:D].astype(jnp.float32),
            )
        )

    for copy in along:
        copy.wait_recv()
    total = z_slots[0].astype(jnp.float32)
    for z in range(1, 8):
        total = total + z_slots[z].astype(jnp.float32)
    all_slots[plane_me] = total
    gathered = []
    for s in range(1, 8):
        _, peer = plane_peer(s)
        copy = pltpu.make_async_remote_copy(
            src_ref=all_slots.at[plane_me],
            dst_ref=all_slots.at[plane_me],
            send_sem=all_send.at[s - 1],
            recv_sem=all_recv.at[s - 1],
            device_id=peer,
            device_id_type=MESH,
        )
        copy.start()
        gathered.append(copy)

    for p in range(2):
        rows = pl.ds((1 - p) * TOK, TOK)
        for g in range(3):
            backward[3 * p + g].wait_recv()
        got = dot(put_remote[...], ret_recv[p])
        first, second = own_parts[p]
        grad_out[rows, 0:128] = low(first + got[0:TOK])
        rest = got[TOK : 2 * TOK] + pltpu.roll(got[2 * TOK :], 64, 1)
        grad_out[rows, 128:D] = low(second + rest[:, 0 : D - 128])

    table_out[...] = jnp.zeros((HEADS, REL), jnp.float32)
    for copy in gathered:
        copy.wait_recv()
    for tile in range(14):
        entries = all_slots[tile // 2, pl.ds(8 * (tile % 2), HEADS), :]
        start = 128 * tile if tile < 7 else 2432 + 128 * (tile - 7)
        size = min(128, REL - start)
        table_out[:, start : start + size] = entries[:, 0:size]

    for copy in forward + backward + reduced + along + gathered:
        copy.wait_send()


def local(n_lon, n_lat, latent, out_grad, gain, shift, qkv_weight, query_bias, proj_weight, bias_table, band_rows):
    del band_rows
    consts = [jnp.asarray(c) for c in constants()]
    args = [
        latent.reshape(2 * TOK, D),
        out_grad.reshape(2 * TOK, D),
        gain.reshape(1, D),
        shift.reshape(1, D),
        qkv_weight,
        query_bias.reshape(1, D),
        proj_weight,
        bias_table.reshape(HEADS, REL),
    ] + consts
    bf16, f32 = jnp.bfloat16, jnp.float32
    dma = pltpu.SemaphoreType.DMA
    scratch = [pltpu.VMEM(a.shape, a.dtype) for a in args] + [
        pltpu.VMEM((2, FWD_ROWS, 128), bf16),
        pltpu.VMEM((2, FWD_ROWS, 128), bf16),
        pltpu.VMEM((2, RET_ROWS, 128), bf16),
        pltpu.VMEM((2, RET_ROWS, 128), bf16),
        pltpu.VMEM((2, 3 * BOTH, 128), f32),
        pltpu.VMEM((2, WTOK, LANES), f32),
        pltpu.VMEM((8, WIDE), f32),
        pltpu.VMEM((2, 64, 128), f32),
        pltpu.VMEM((8, 256), f32),
        pltpu.VMEM((256, LANES), bf16),
        pltpu.VMEM((256, 256), bf16),
        pltpu.VMEM((LANES, 256), bf16),
        pltpu.VMEM((LANES, 256), bf16),
        pltpu.VMEM((2, BOTH, 256), bf16),
        pltpu.VMEM((8, 16, 128), bf16),
        pltpu.VMEM((7, 16, 128), bf16),
        pltpu.VMEM((8, 16, 128), bf16),
        pltpu.VMEM((8, 16, 128), f32),
        dma((len(args),)),
        dma((2, 3)),
        dma((2, 3)),
        dma((2, 3)),
        dma((2, 3)),
        dma((7,)),
        dma((7,)),
        dma((7,)),
        dma((7,)),
        dma((7,)),
        dma((7,)),
    ]
    grad, table = pl.pallas_call(
        functools.partial(kernel, n_lon, n_lat, len(args)),
        out_shape=(
            jax.ShapeDtypeStruct((2 * TOK, D), bf16),
            jax.ShapeDtypeStruct((HEADS, REL), f32),
        ),
        in_specs=[pl.BlockSpec(memory_space=pl.ANY)] * len(args),
        out_specs=(pl.BlockSpec(memory_space=pltpu.VMEM), pl.BlockSpec(memory_space=pltpu.VMEM)),
        scratch_shapes=scratch,
        compiler_params=pltpu.CompilerParams(
            collective_id=0, has_side_effects=True, vmem_limit_bytes=50 * 1024 * 1024
        ),
    )(*args)
    return grad.reshape(latent.shape), table.reshape(bias_table.shape)


def solution(mesh):
    in_specs = (
        P(None, "lat", "lon", None),
        P(None, "lat", "lon", None),
        P(),
        P(),
        P(),
        P(),
        P(),
        P("lat", None, None, None),
        P("lat"),
    )
    out_specs = (P(None, "lat", "lon", None), P("lat", None, None, None))
    body = functools.partial(local, mesh.shape["lon"], mesh.shape["lat"])
    return jax.shard_map(body, mesh=mesh, in_specs=in_specs, out_specs=out_specs, check_vma=False)
```

```python
import functools

import jax
import jax.numpy as jnp
import ml_dtypes
import numpy as np
from jax import lax
from jax.experimental import pallas as pl
from jax.experimental.pallas import tpu as pltpu
from jax.sharding import PartitionSpec as P

HEADS = 6
D = 192
WLAT = 6
WLON = 12
ROWS = 6
COLS = 24
REL = 3312
SPAN = 2 * WLON - 1
FLAT = SPAN * WLAT * WLAT
EPSILON = 1e-05
SCALE = 32 ** (-0.5)
TOK = ROWS * COLS
WTOK = 96
BOTH = 2 * WTOK
FWD = ((0, 336), (336, 112), (448, 336), (784, 112))
FWD_ROWS = 896
FWD_CUT = (176, 64)
RET = ((0, 96), (96, 32), (128, 96), (224, 32))
RET_ROWS = 256
LANES = HEADS * 128
WIDE = 896
MASKED = -1e30
MESH = pl.DeviceIdType.MESH


def constants():
    def token(row, col):
        return row * COLS + col

    def wrow(rolled_row, rolled_col):
        return (rolled_col // WLON) * WTOK + (rolled_col % WLON) * 8 + rolled_row

    groups = [
        [
            (token(r, c), wrow((r + 3) % ROWS, (c + 18) % COLS))
            for r in rows
            for c in cols
        ]
        for rows in (range(3, ROWS), range(3))
        for cols in (range(6, COLS), range(6))
    ]

    pack = np.zeros((FWD_ROWS, 6 * TOK), np.float32)
    take_remote = np.zeros((2, 3 * BOTH, 480), np.float32)
    ret_pack = np.zeros((RET_ROWS, 3 * BOTH), np.float32)
    put_remote = np.zeros((3 * TOK, RET_ROWS), np.float32)
    for quarter, ((at, _), (back, _), group) in enumerate(zip(FWD, RET, groups)):
        n = len(group)
        for k, (t, w) in enumerate(group):
            for p in range(2):
                for part in range(3):
                    row = (3 * p + part) * n + k
                    pack[at + row, (3 * p + part) * TOK + t] = 1
                    seen = row - p * (FWD_CUT[quarter % 2] - 16)
                    take_remote[p, part * BOTH + w, (0, 176, 240, 416)[quarter] + seen] = 1
            ret_pack[back + k, w] = 1
            put_remote[t, back + k] = 1
            high = k >= n // 2
            slot = back + n + k % (n // 2)
            ret_pack[slot, (2 if high else 1) * BOTH + w] = 1
            put_remote[(2 if high else 1) * TOK + t, slot] = 1
    tails = np.zeros((2, D, 128), np.float32)
    for i in range(64):
        tails[0, 128 + i, i] = 1
        tails[1, 128 + i, 64 + i] = 1
    spread = np.zeros((256, WIDE), np.float32)
    for d in range(SPAN):
        for a in range(WLAT):
            spread[8 * d + a, SPAN * WLAT * a + d] = 1
    qkv_pad = np.zeros((3 * D, LANES), np.float32)
    for part in range(3):
        for i in range(D):
            qkv_pad[part * D + i, part * 256 + i] = 1
    proj_pad = np.zeros((D, 256), np.float32)
    for i in range(D):
        proj_pad[i, i if i < 128 else 64 + i] = 1
    head_mask = np.zeros((16, 256), np.float32)
    for h in range(HEADS):
        head_mask[h, h * 32 : (h + 1) * 32] = 1
    matrices = (
        pack,
        tails.reshape(2 * D, 128),
        take_remote.reshape(6 * BOTH, 480),
        ret_pack,
        put_remote,
        spread,
        qkv_pad,
        proj_pad,
        head_mask,
    )
    return tuple(m.astype(ml_dtypes.bfloat16) for m in matrices)


def dot(a, b):
    return jnp.dot(a, b, preferred_element_type=jnp.float32)


def dot_nt(a, b):
    return lax.dot_general(a, b, (((1,), (1,)), ((), ())), preferred_element_type=jnp.float32)


def dot_tn(a, b):
    return lax.dot_general(a, b, (((0,), (0,)), ((), ())), preferred_element_type=jnp.float32)


def low(a):
    return a.astype(jnp.bfloat16)


def kernel(n_lon, n_lat, n_in, *refs):
    ins, refs = refs[:n_in], refs[n_in:]
    (grad_out, table_out), refs = refs[:2], refs[2:]
    held, refs = refs[:n_in], refs[n_in:]
    (
        send_buf,
        recv_buf,
        ret_send,
        ret_recv,
        bias,
        table_pad,
        fold_buf,
        vecs,
        w_qkv,
        w_proj,
        q_heads,
        u_heads,
        red_src,
        red_in,
        z_slots,
        all_slots,
        in_sem,
        fwd_send,
        fwd_recv,
        back_send,
        back_recv,
        red_send,
        red_recv,
        z_send,
        z_recv,
        all_send,
        all_recv,
        ready,
    ) = refs
    (
        latent,
        out_grad,
        gain,
        shift,
        qkv_weight,
        query_bias,
        proj_weight,
        bias_table,
        pack,
        tails,
        take_remote,
        ret_pack,
        put_remote,
        spread,
        qkv_pad,
        proj_pad,
        head_mask,
    ) = held

    lon, lat = lax.axis_index("lon"), lax.axis_index("lat")
    lon_m = lax.rem(lon + n_lon - 1, n_lon)
    lat_m, lat_p = lax.rem(lat + n_lat - 1, n_lat), lax.rem(lat + 1, n_lat)

    def at(lon_at, lat_at):
        return {"lon": lon_at, "lat": lat_at}

    def half_way(strip):
        return (strip // 16) * 16 + lax.rem(strip + 8, 16)

    job = half_way(lon)
    job_p = lax.rem(job + 1, n_lon)
    workers = (
        at(half_way(lon), lat),
        at(half_way(lon_m), lat),
        at(half_way(lon), lat_m),
        at(half_way(lon_m), lat_m),
    )
    homes = (at(job, lat), at(job_p, lat), at(job, lat_p), at(job_p, lat_p))
    z_me = lax.rem(lon // 2, 8)
    y_me = lon // 16
    plane_me = y_me * 2 + lax.rem(lon, 2)

    def plane_peer(step):
        rank = lax.rem(plane_me + step, 8)
        return rank, at(((rank // 2) * 8 + z_me) * 2 + lax.rem(rank, 2), lat)

    def z_peer(step):
        z = lax.rem(z_me + step, 8)
        return at((y_me * 8 + z) * 2 + lax.rem(lon, 2), lat)

    z_ring = lax.rem(lat, 2) * 8 + z_me

    def ring_peer(step):
        z = lax.rem(z_ring + step + 16, 16)
        return at((y_me * 8 + lax.rem(z, 8)) * 2 + lax.rem(lon, 2), (lat // 2) * 2 + z // 8)

    barrier = pltpu.get_barrier_semaphore()
    everyone = list(workers) + list(homes)
    everyone += [ring_peer(s) for s in range(-4, 5) if s] + [plane_peer(s)[1] for s in range(1, 8)]
    for peer in everyone:
        pl.semaphore_signal(barrier, inc=1, device_id=peer, device_id_type=MESH)

    loads = [pltpu.make_async_copy(s, d, in_sem.at[i]) for i, (s, d) in enumerate(zip(ins, held))]
    order = [0, 1, 9, 8, 4, 14, 6, 15, 13, 7, 2, 3, 5, 16, 10, 11, 12]
    for i in order:
        loads[i].start()
    for i in (0, 1, 9, 8):
        loads[i].wait()

    source = []
    for p in range(2):
        rows = pl.ds((1 - p) * TOK, TOK)
        mixed = dot(latent[rows, :], tails[0:D, :]) + dot(out_grad[rows, :], tails[D : 2 * D, :])
        source += [latent[rows, 0:128], out_grad[rows, 0:128], low(mixed)]
    send_buf[...] = low(dot(pack[...], jnp.concatenate(source, 0)))

    pl.semaphore_wait(barrier, len(everyone))
    for step in (-4, 4):
        pl.semaphore_signal(ready, inc=1, device_id=ring_peer(step), device_id_type=MESH)
    upper = lax.rem(lat, 2)

    def pick(k, places):
        here, there = places[k], places[(k + 2) % 4]
        return {name: jnp.where(upper == 0, here[name], there[name]) for name in here}

    def forward(p, k, moved):
        q = lax.rem(k + 2 * upper, 4) if moved else k
        cut = FWD_CUT[k % 2]
        size = cut if p == 0 else FWD[k][1] - cut
        start = pl.multiple_of((q // 2) * FWD[2][0] + FWD[k % 2][0] + p * cut, 16)
        return pltpu.make_async_remote_copy(
            src_ref=send_buf.at[pl.ds(start, size)],
            dst_ref=recv_buf.at[pl.ds(start, size)],
            send_sem=fwd_send.at[p, q],
            recv_sem=fwd_recv.at[p, q],
            device_id=pick(k, workers) if moved else workers[k],
            device_id_type=MESH,
        )

    def backward(p, k, moved):
        q = lax.rem(k + 2 * upper, 4) if moved else k
        start = pl.multiple_of((q // 2) * RET[2][0] + RET[k % 2][0], 16)
        return pltpu.make_async_remote_copy(
            src_ref=ret_send.at[p, pl.ds(start, RET[k][1])],
            dst_ref=ret_recv.at[p, pl.ds(start, RET[k][1])],
            send_sem=back_send.at[p, q],
            recv_sem=back_recv.at[p, q],
            device_id=pick(k, homes) if moved else homes[k],
            device_id_type=MESH,
        )

    for ks in ((0, 1), (2, 3)):
        for p in range(2):
            for k in ks:
                forward(p, k, True).start()

    for i in order:
        if i not in (0, 1, 9, 8):
            loads[i].wait()

    w_qkv[0:D, :] = low(dot(qkv_weight[...], qkv_pad[...]))
    w_qkv[D:256, :] = jnp.zeros((256 - D, LANES), jnp.bfloat16)
    w_proj[0:D, :] = low(dot(proj_weight[...], proj_pad[...]))
    w_proj[D:256, :] = jnp.zeros((256 - D, 256), jnp.bfloat16)
    vecs[...] = jnp.zeros((8, 256), jnp.float32)
    vecs[0:1, 0:D] = gain[...]
    vecs[1:2, 0:D] = shift[...]
    vecs[2:3, 0:D] = query_bias[...]
    for h in range(HEADS):
        pad = pl.ds(h * 128 + WTOK, 128 - WTOK)
        q_heads[:, pad, :] = jnp.zeros((4, 128 - WTOK, 256), jnp.bfloat16)
        u_heads[:, pad, :] = jnp.zeros((4, 128 - WTOK, 256), jnp.bfloat16)

    lane8 = lax.broadcasted_iota(jnp.int32, (8, 128), 1)
    row8 = lax.broadcasted_iota(jnp.int32, (8, 128), 0)
    last = (lat == n_lat - 1).astype(jnp.int32)
    query_half = (lax.rem(lane8, 8) >= 3).astype(jnp.int32)
    key_half = (row8 >= 3).astype(jnp.int32)
    left_out = (row8 >= WLAT).astype(jnp.int32) + last * (query_half ^ key_half) > 0

    for p in range(2):
        table_pad[...] = jnp.zeros((8, WIDE), jnp.float32)
        if p == 0:
            for h in range(HEADS):
                table_pad[h : h + 1, :] = bias_table[h, :, 0:WIDE]
        else:
            for h in range(HEADS):
                table_pad[h : h + 1, 0 : REL - 2432] = bias_table[h, :, 2432:REL]
        entries = table_pad[...]
        for b in range(8):
            if b < WLAT:
                moved = pltpu.roll(entries, (2 * WIDE - SPAN * b - 52 * p) % WIDE, 1)
                top = low(moved)
                rest = low(moved - top.astype(jnp.float32))
                row = dot_nt(top, spread[...]) + dot_nt(rest, spread[...])
            else:
                row = jnp.zeros((8, 256), jnp.float32)
            fold_buf[0, 8 * b : 8 * b + 8, :] = row[:, 0:128]
            fold_buf[1, 8 * b : 8 * b + 8, :] = row[:, 128:256]
        for h in range(HEADS):
            near = fold_buf[0, pl.ds(h, 8, stride=8), :]
            far = fold_buf[1, pl.ds(h, 8, stride=8), :]
            for r in range(WLON):
                s = 8 * (WLON - 1 - r)
                if s:
                    block = pltpu.roll(jnp.where(lane8 >= s, near, far), 128 - s, 1)
                else:
                    block = near
                bias[p, 8 * r : 8 * r + 8, 128 * h : 128 * h + 128] = jnp.where(left_out, MASKED, block)

    gain_w, shift_w, query_w = vecs[0:1, :], vecs[1:2, :], vecs[2:3, :]
    below64 = lax.broadcasted_iota(jnp.int32, (BOTH, 128), 1) < 64
    low_lane = lax.broadcasted_iota(jnp.int32, (BOTH, 256), 1) < D
    flats = []
    kept = []

    def send_back(p):
        per_window, normed, inverse = kept[p]
        rows = []
        for w, (prob_low, score_low, key_w) in enumerate(per_window):
            value_g = dot(prob_low, u_heads[2 * p + w])
            key_g = dot(score_low, q_heads[2 * p + w]) * SCALE
            query_all = dot_tn(score_low, key_w)
            query_g = None
            for h in range(HEADS):
                term = query_all[h * 128 : h * 128 + WTOK] * head_mask[h : h + 1, :].astype(jnp.float32)
                query_g = term if query_g is None else query_g + term
            rows.append(jnp.concatenate([low(query_g * SCALE), low(key_g), low(value_g)], 1))
        hidden_grad = dot_nt(jnp.concatenate(rows, 0), w_qkv[...])
        scaled = hidden_grad * gain_w
        mean_g = jnp.sum(scaled, 1, keepdims=True) * (1.0 / D)
        mean_gn = jnp.sum(scaled * normed, 1, keepdims=True) * (1.0 / D)
        branch = jnp.where(low_lane, inverse * (scaled - mean_g - normed * mean_gn), 0.0)
        second = branch[:, 128:256]
        stacked = jnp.concatenate([branch[:, 0:128], second, pltpu.roll(second, 64, 1)], 0)
        ret_send[p] = low(dot(ret_pack[...], low(stacked)))
        for k in range(2):
            backward(p, k, True).start()


    for p in range(2):
        for k in range(4):
            forward(p, k, False).wait_recv()
        got = [
            recv_buf[pl.ds(FWD[k][0] + p * (FWD_CUT[k % 2] - 16), FWD_CUT[k % 2]), :] for k in range(4)
        ]
        tokens = dot(take_remote[pl.ds(3 * BOTH * p, 3 * BOTH), :], jnp.concatenate(got, 0))
        x_a, x_b, x_c = tokens[0:BOTH], tokens[BOTH : 2 * BOTH], tokens[2 * BOTH :]
        tail = jnp.where(below64, x_c, 0.0)
        center = (jnp.sum(x_a, 1, keepdims=True) + jnp.sum(tail, 1, keepdims=True)) * (1.0 / D)
        c_a = x_a - center
        c_t = jnp.where(below64, x_c - center, 0.0)
        spread_sq = (
            jnp.sum(c_a * c_a, 1, keepdims=True) + jnp.sum(c_t * c_t, 1, keepdims=True)
        ) * (1.0 / D)
        inverse = lax.rsqrt(spread_sq + EPSILON)
        normed = jnp.concatenate([c_a, c_t], 1) * inverse
        hidden = low(normed * gain_w + shift_w)
        projected = dot(hidden, w_qkv[...])
        queries = low(projected[:, 0:256] + query_w)
        keys = low(projected[:, 256:512])
        values = low(projected[:, 512:768])
        incoming = low(jnp.concatenate([x_b, x_c], 1))
        upstream = low(dot_nt(incoming, w_proj[...]))

        per_window = []
        score_sum = None
        for w in range(2):
            span = slice(w * WTOK, (w + 1) * WTOK)
            q_w, u_w = q_heads.at[2 * p + w], u_heads.at[2 * p + w]
            for h in range(HEADS):
                mask = head_mask[h : h + 1, :]
                q_w[pl.ds(h * 128, WTOK), :] = queries[span] * mask
                u_w[pl.ds(h * 128, WTOK), :] = upstream[span] * mask
            scores = dot_nt(keys[span], q_w[...]) * SCALE + bias[p]
            weights = jnp.exp(scores)
            probs = weights * (1.0 / jnp.sum(weights, 0, keepdims=True))
            prob_grad = dot_nt(values[span], u_w[...])
            inner = jnp.sum(probs * prob_grad, 0, keepdims=True)
            score_grad = probs * (prob_grad - inner)
            score_sum = score_grad if score_sum is None else score_sum + score_grad
            per_window.append((low(probs), low(score_grad), keys[span]))
        kept.append((per_window, normed, inverse))

        for h in range(HEADS):
            near = far = None
            for r in range(WLON):
                s = 8 * (WLON - 1 - r)
                block = score_sum[8 * r : 8 * r + 8, 128 * h : 128 * h + 128]
                if s:
                    block = pltpu.roll(block, s, 1)
                    wrapped = jnp.where(lane8 < s, block, 0.0)
                    block = jnp.where(lane8 < s, 0.0, block)
                    far = wrapped if far is None else far + wrapped
                near = block if near is None else near + block
            fold_buf[0, 8 * h : 8 * h + 8, :] = near
            fold_buf[1, 8 * h : 8 * h + 8, :] = far
        by_row = [
            jnp.concatenate([fold_buf[part, pl.ds(b, 8, stride=8), :] for part in range(2)], 1)
            for b in range(WLAT)
        ]
        lines = dot(low(jnp.concatenate(by_row, 0)), spread[...])
        flat = None
        for b in range(WLAT):
            line = lines[8 * b : 8 * b + 8]
            if b or p:
                line = pltpu.roll(line, SPAN * b + 52 * p, 1)
            flat = line if flat is None else flat + line
        flats.append(flat)
        if p == 0:
            send_back(0)

    for c in range(8):
        for half in range(2):
            tile = 2 * c + half
            if tile < 14:
                part = flats[tile // 7][:, 128 * (tile % 7) : 128 * (tile % 7) + 128]
            else:
                part = jnp.zeros((8, 128), jnp.float32)
            all_slots[c, 8 * half : 8 * half + 8, :] = part
        red_src[c] = low(all_slots[c])
    reduced = []
    for s in range(1, 8):
        rank, peer = plane_peer(s)
        copy = pltpu.make_async_remote_copy(
            src_ref=red_src.at[rank],
            dst_ref=red_in.at[s - 1],
            send_sem=red_send.at[s - 1],
            recv_sem=red_recv.at[s - 1],
            device_id=peer,
            device_id_type=MESH,
        )
        copy.start()
        reduced.append(copy)

    send_back(1)
    for copy in reduced:
        copy.wait_recv()
    total = red_src[plane_me].astype(jnp.float32)
    for s in range(7):
        total = total + red_in[s].astype(jnp.float32)
    z_slots[z_me] = low(total)
    pl.semaphore_wait(ready, 2)
    along = []
    for s in range(1, 8):
        copy = pltpu.make_async_remote_copy(
            src_ref=z_slots.at[z_me],
            dst_ref=z_slots.at[z_me],
            send_sem=z_send.at[s - 1],
            recv_sem=z_recv.at[s - 1],
            device_id=z_peer(s),
            device_id_type=MESH,
        )
        copy.start()
        along.append(copy)

    for p in range(2):
        for k in range(2, 4):
            backward(p, k, True).start()

    for copy in along:
        copy.wait_recv()
    total = z_slots[0].astype(jnp.float32)
    for z in range(1, 8):
        total = total + z_slots[z].astype(jnp.float32)
    all_slots[plane_me] = total
    gathered = []
    for s in range(1, 8):
        _, peer = plane_peer(s)
        copy = pltpu.make_async_remote_copy(
            src_ref=all_slots.at[plane_me],
            dst_ref=all_slots.at[plane_me],
            send_sem=all_send.at[s - 1],
            recv_sem=all_recv.at[s - 1],
            device_id=peer,
            device_id_type=MESH,
        )
        copy.start()
        gathered.append(copy)

    for p in range(2):
        rows = pl.ds((1 - p) * TOK, TOK)
        for k in range(4):
            backward(p, k, False).wait_recv()
        got = dot(put_remote[...], ret_recv[p])
        rest = got[TOK : 2 * TOK] + pltpu.roll(got[2 * TOK :], 64, 1)
        grad_out[rows, 0:128] = low(out_grad[rows, 0:128].astype(jnp.float32) + got[0:TOK])
        grad_out[rows, 128:D] = low(out_grad[rows, 128:D].astype(jnp.float32) + rest[:, 0 : D - 128])

    table_out[...] = jnp.zeros((HEADS, 1, REL), jnp.float32)
    for copy in gathered:
        copy.wait_recv()
    for tile in range(14):
        start = 128 * tile if tile < 7 else 2432 + 128 * (tile - 7)
        size = min(128, REL - start)
        for h in range(HEADS):
            entries = all_slots[tile // 2, pl.ds(8 * (tile % 2) + h, 1), :]
            table_out[h, :, start : start + size] = entries[:, 0:size]

    for p in range(2):
        for k in range(4):
            forward(p, k, False).wait_send()
            backward(p, k, False).wait_send()
    for copy in reduced + along + gathered:
        copy.wait_send()


def local(n_lon, n_lat, latent, out_grad, gain, shift, qkv_weight, query_bias, proj_weight, bias_table, band_rows):
    del band_rows
    consts = [jnp.asarray(c) for c in constants()]
    args = [
        latent.reshape(2 * TOK, D),
        out_grad.reshape(2 * TOK, D),
        gain.reshape(1, D),
        shift.reshape(1, D),
        qkv_weight,
        query_bias.reshape(1, D),
        proj_weight,
        bias_table.reshape(HEADS, 1, REL),
    ] + consts
    bf16, f32 = jnp.bfloat16, jnp.float32
    dma = pltpu.SemaphoreType.DMA
    scratch = [pltpu.VMEM(a.shape, a.dtype) for a in args] + [
        pltpu.VMEM((FWD_ROWS, 128), bf16),
        pltpu.VMEM((FWD_ROWS, 128), bf16),
        pltpu.VMEM((2, RET_ROWS, 128), bf16),
        pltpu.VMEM((2, RET_ROWS, 128), bf16),
        pltpu.VMEM((2, WTOK, LANES), f32),
        pltpu.VMEM((8, WIDE), f32),
        pltpu.VMEM((2, 64, 128), f32),
        pltpu.VMEM((8, 256), f32),
        pltpu.VMEM((256, LANES), bf16),
        pltpu.VMEM((256, 256), bf16),
        pltpu.VMEM((4, LANES, 256), bf16),
        pltpu.VMEM((4, LANES, 256), bf16),
        pltpu.VMEM((8, 16, 128), bf16),
        pltpu.VMEM((7, 16, 128), bf16),
        pltpu.VMEM((8, 16, 128), bf16),
        pltpu.VMEM((8, 16, 128), f32),
        dma((len(args),)),
        dma((2, 4)),
        dma((2, 4)),
        dma((2, 4)),
        dma((2, 4)),
        dma((7,)),
        dma((7,)),
        dma((7,)),
        dma((7,)),
        dma((7,)),
        dma((7,)),
        pltpu.SemaphoreType.REGULAR,
    ]
    grad, table = pl.pallas_call(
        functools.partial(kernel, n_lon, n_lat, len(args)),
        out_shape=(
            jax.ShapeDtypeStruct((2 * TOK, D), bf16),
            jax.ShapeDtypeStruct((HEADS, 1, REL), f32),
        ),
        in_specs=[pl.BlockSpec(memory_space=pltpu.HBM)] * len(args),
        out_specs=(pl.BlockSpec(memory_space=pltpu.VMEM), pl.BlockSpec(memory_space=pltpu.VMEM)),
        scratch_shapes=scratch,
        compiler_params=pltpu.CompilerParams(
            collective_id=0, has_side_effects=True, vmem_limit_bytes=63 * 1024 * 1024
        ),
    )(*args)
    return grad.reshape(latent.shape), table.reshape(bias_table.shape)


def solution(mesh):
    in_specs = (
        P(None, "lat", "lon", None),
        P(None, "lat", "lon", None),
        P(),
        P(),
        P(),
        P(),
        P(),
        P("lat", None, None, None),
        P("lat"),
    )
    out_specs = (P(None, "lat", "lon", None), P("lat", None, None, None))
    body = functools.partial(local, mesh.shape["lon"], mesh.shape["lat"])
    return jax.shard_map(body, mesh=mesh, in_specs=in_specs, out_specs=out_specs, check_vma=False)
```

```python
import functools

import jax
import jax.numpy as jnp
import ml_dtypes
import numpy as np
from jax import lax
from jax.experimental import pallas as pl
from jax.experimental.pallas import tpu as pltpu
from jax.sharding import PartitionSpec as P

HEADS = 6
D = 192
WLAT = 6
WLON = 12
ROWS = 6
COLS = 24
REL = 3312
SPAN = 2 * WLON - 1
FLAT = SPAN * WLAT * WLAT
EPSILON = 1e-05
SCALE = 32 ** (-0.5)
TOK = ROWS * COLS
WTOK = 96
BOTH = 2 * WTOK
FWD = ((0, 336), (336, 112), (448, 336), (784, 112))
FWD_ROWS = 896
FWD_CUT = (176, 64)
RET = ((0, 96), (96, 32), (128, 96), (224, 32))
RET_ROWS = 256
LANES = HEADS * 128
WIDE = 896
MASKED = -1e30
MESH = pl.DeviceIdType.MESH


def constants():
    def token(row, col):
        return row * COLS + col

    def wrow(rolled_row, rolled_col):
        return (rolled_col // WLON) * WTOK + (rolled_col % WLON) * 8 + rolled_row

    groups = [
        [
            (token(r, c), wrow((r + 3) % ROWS, (c + 18) % COLS))
            for r in rows
            for c in cols
        ]
        for rows in (range(3, ROWS), range(3))
        for cols in (range(6, COLS), range(6))
    ]

    pack = np.zeros((FWD_ROWS, 6 * TOK), np.float32)
    take_remote = np.zeros((2, 3 * BOTH, 480), np.float32)
    ret_pack = np.zeros((RET_ROWS, 3 * BOTH), np.float32)
    put_remote = np.zeros((3 * TOK, RET_ROWS), np.float32)
    for quarter, ((at, _), (back, _), group) in enumerate(zip(FWD, RET, groups)):
        n = len(group)
        for k, (t, w) in enumerate(group):
            for p in range(2):
                for part in range(3):
                    row = (3 * p + part) * n + k
                    pack[at + row, (3 * p + part) * TOK + t] = 1
                    seen = row - p * (FWD_CUT[quarter % 2] - 16)
                    take_remote[p, part * BOTH + w, (0, 176, 240, 416)[quarter] + seen] = 1
            ret_pack[back + k, w] = 1
            put_remote[t, back + k] = 1
            high = k >= n // 2
            slot = back + n + k % (n // 2)
            ret_pack[slot, (2 if high else 1) * BOTH + w] = 1
            put_remote[(2 if high else 1) * TOK + t, slot] = 1
    tails = np.zeros((2, D, 128), np.float32)
    for i in range(64):
        tails[0, 128 + i, i] = 1
        tails[1, 128 + i, 64 + i] = 1
    spread = np.zeros((256, WIDE), np.float32)
    for d in range(SPAN):
        for a in range(WLAT):
            spread[8 * d + a, SPAN * WLAT * a + d] = 1
    qkv_pad = np.zeros((3 * D, LANES), np.float32)
    for part in range(3):
        for i in range(D):
            qkv_pad[part * D + i, part * 256 + i] = 1
    proj_pad = np.zeros((D, 256), np.float32)
    for i in range(D):
        proj_pad[i, i if i < 128 else 64 + i] = 1
    head_mask = np.zeros((16, 256), np.float32)
    for h in range(HEADS):
        head_mask[h, h * 32 : (h + 1) * 32] = 1
    matrices = (
        pack,
        tails.reshape(2 * D, 128),
        take_remote.reshape(6 * BOTH, 480),
        ret_pack,
        put_remote,
        spread,
        qkv_pad,
        proj_pad,
        head_mask,
    )
    return tuple(m.astype(ml_dtypes.bfloat16) for m in matrices)


def dot(a, b):
    return jnp.dot(a, b, preferred_element_type=jnp.float32)


def dot_nt(a, b):
    return lax.dot_general(a, b, (((1,), (1,)), ((), ())), preferred_element_type=jnp.float32)


def dot_tn(a, b):
    return lax.dot_general(a, b, (((0,), (0,)), ((), ())), preferred_element_type=jnp.float32)


def low(a):
    return a.astype(jnp.bfloat16)


def kernel(n_lon, n_lat, n_in, *refs):
    ins, refs = refs[:n_in], refs[n_in:]
    (grad_out, all_slots), refs = refs[:2], refs[2:]
    held, refs = refs[:n_in], refs[n_in:]
    (
        send_buf,
        recv_buf,
        ret_send,
        ret_recv,
        bias,
        table_pad,
        fold_buf,
        vecs,
        w_qkv,
        w_proj,
        q_heads,
        u_heads,
        red_src,
        red_in,
        z_slots,
        final,
        grad_held,
        out_sem,
        in_sem,
        fwd_send,
        fwd_recv,
        back_send,
        back_recv,
        red_send,
        red_recv,
        z_send,
        z_recv,
        all_send,
        all_recv,
        ready,
    ) = refs
    (
        latent,
        out_grad,
        gain,
        shift,
        qkv_weight,
        query_bias,
        proj_weight,
        bias_table,
        pack,
        tails,
        take_remote,
        ret_pack,
        put_remote,
        spread,
        qkv_pad,
        proj_pad,
        head_mask,
    ) = held

    lon, lat = lax.axis_index("lon"), lax.axis_index("lat")
    lon_m = lax.rem(lon + n_lon - 1, n_lon)
    lat_m, lat_p = lax.rem(lat + n_lat - 1, n_lat), lax.rem(lat + 1, n_lat)

    def at(lon_at, lat_at):
        return {"lon": lon_at, "lat": lat_at}

    def half_way(strip):
        return (strip // 16) * 16 + lax.rem(strip + 8, 16)

    job = half_way(lon)
    job_p = lax.rem(job + 1, n_lon)
    workers = (
        at(half_way(lon), lat),
        at(half_way(lon_m), lat),
        at(half_way(lon), lat_m),
        at(half_way(lon_m), lat_m),
    )
    homes = (at(job, lat), at(job_p, lat), at(job, lat_p), at(job_p, lat_p))
    z_me = lax.rem(lon // 2, 8)
    y_me = lon // 16
    plane_me = y_me * 2 + lax.rem(lon, 2)

    def plane_peer(step):
        rank = lax.rem(plane_me + step, 8)
        return rank, at(((rank // 2) * 8 + z_me) * 2 + lax.rem(rank, 2), lat)

    def z_peer(step):
        z = lax.rem(z_me + step, 8)
        return at((y_me * 8 + z) * 2 + lax.rem(lon, 2), lat)

    z_ring = lax.rem(lat, 2) * 8 + z_me

    def ring_peer(step):
        z = lax.rem(z_ring + step + 16, 16)
        return at((y_me * 8 + lax.rem(z, 8)) * 2 + lax.rem(lon, 2), (lat // 2) * 2 + z // 8)

    barrier = pltpu.get_barrier_semaphore()
    everyone = list(workers) + list(homes)
    everyone += [ring_peer(s) for s in range(-4, 5) if s] + [plane_peer(s)[1] for s in range(1, 8)]
    for peer in everyone:
        pl.semaphore_signal(barrier, inc=1, device_id=peer, device_id_type=MESH)

    loads = [pltpu.make_async_copy(s, d, in_sem.at[i]) for i, (s, d) in enumerate(zip(ins, held))]
    order = [0, 1, 9, 8, 4, 14, 6, 15, 13, 7, 2, 3, 5, 16, 10, 11, 12]
    for i in order:
        loads[i].start()
    for i in (0, 1, 9, 8):
        loads[i].wait()

    source = []
    for p in range(2):
        rows = pl.ds((1 - p) * TOK, TOK)
        mixed = dot(latent[rows, :], tails[0:D, :]) + dot(out_grad[rows, :], tails[D : 2 * D, :])
        source += [latent[rows, 0:128], out_grad[rows, 0:128], low(mixed)]
    send_buf[...] = low(dot(pack[...], jnp.concatenate(source, 0)))

    pl.semaphore_wait(barrier, len(everyone))
    for step in (-4, 4):
        pl.semaphore_signal(ready, inc=1, device_id=ring_peer(step), device_id_type=MESH)
    upper = lax.rem(lat, 2)

    def pick(k, places):
        here, there = places[k], places[(k + 2) % 4]
        return {name: jnp.where(upper == 0, here[name], there[name]) for name in here}

    def forward(p, k, moved):
        q = lax.rem(k + 2 * upper, 4) if moved else k
        cut = FWD_CUT[k % 2]
        size = cut if p == 0 else FWD[k][1] - cut
        start = pl.multiple_of((q // 2) * FWD[2][0] + FWD[k % 2][0] + p * cut, 16)
        return pltpu.make_async_remote_copy(
            src_ref=send_buf.at[pl.ds(start, size)],
            dst_ref=recv_buf.at[pl.ds(start, size)],
            send_sem=fwd_send.at[p, q],
            recv_sem=fwd_recv.at[p, q],
            device_id=pick(k, workers) if moved else workers[k],
            device_id_type=MESH,
        )

    def backward(p, k, moved):
        q = lax.rem(k + 2 * upper, 4) if moved else k
        start = pl.multiple_of((q // 2) * RET[2][0] + RET[k % 2][0], 16)
        return pltpu.make_async_remote_copy(
            src_ref=ret_send.at[p, pl.ds(start, RET[k][1])],
            dst_ref=ret_recv.at[p, pl.ds(start, RET[k][1])],
            send_sem=back_send.at[p, q],
            recv_sem=back_recv.at[p, q],
            device_id=pick(k, homes) if moved else homes[k],
            device_id_type=MESH,
        )

    for ks in ((0, 1), (2, 3)):
        for p in range(2):
            for k in ks:
                forward(p, k, True).start()

    for i in order:
        if i not in (0, 1, 9, 8):
            loads[i].wait()

    w_qkv[0:D, :] = low(dot(qkv_weight[...], qkv_pad[...]))
    w_qkv[D:256, :] = jnp.zeros((256 - D, LANES), jnp.bfloat16)
    w_proj[0:D, :] = low(dot(proj_weight[...], proj_pad[...]))
    w_proj[D:256, :] = jnp.zeros((256 - D, 256), jnp.bfloat16)
    vecs[...] = jnp.zeros((8, 256), jnp.float32)
    vecs[0:1, 0:D] = gain[...]
    vecs[1:2, 0:D] = shift[...]
    vecs[2:3, 0:D] = query_bias[...]
    for h in range(HEADS):
        pad = pl.ds(h * 128 + WTOK, 128 - WTOK)
        q_heads[:, pad, :] = jnp.zeros((4, 128 - WTOK, 256), jnp.bfloat16)
        u_heads[:, pad, :] = jnp.zeros((4, 128 - WTOK, 256), jnp.bfloat16)

    lane8 = lax.broadcasted_iota(jnp.int32, (8, 128), 1)
    row8 = lax.broadcasted_iota(jnp.int32, (8, 128), 0)
    last = (lat == n_lat - 1).astype(jnp.int32)
    query_half = (lax.rem(lane8, 8) >= 3).astype(jnp.int32)
    key_half = (row8 >= 3).astype(jnp.int32)
    left_out = (row8 >= WLAT).astype(jnp.int32) + last * (query_half ^ key_half) > 0

    for p in range(2):
        table_pad[...] = jnp.zeros((8, WIDE), jnp.float32)
        if p == 0:
            for h in range(HEADS):
                table_pad[h : h + 1, :] = bias_table[h, :, 0:WIDE]
        else:
            for h in range(HEADS):
                table_pad[h : h + 1, 0 : REL - 2432] = bias_table[h, :, 2432:REL]
        entries = table_pad[...]
        for b in range(8):
            if b < WLAT:
                moved = pltpu.roll(entries, (2 * WIDE - SPAN * b - 52 * p) % WIDE, 1)
                top = low(moved)
                rest = low(moved - top.astype(jnp.float32))
                row = dot_nt(top, spread[...]) + dot_nt(rest, spread[...])
            else:
                row = jnp.zeros((8, 256), jnp.float32)
            fold_buf[0, 8 * b : 8 * b + 8, :] = row[:, 0:128]
            fold_buf[1, 8 * b : 8 * b + 8, :] = row[:, 128:256]
        for h in range(HEADS):
            near = fold_buf[0, pl.ds(h, 8, stride=8), :]
            far = fold_buf[1, pl.ds(h, 8, stride=8), :]
            for r in range(WLON):
                s = 8 * (WLON - 1 - r)
                if s:
                    block = pltpu.roll(jnp.where(lane8 >= s, near, far), 128 - s, 1)
                else:
                    block = near
                bias[p, 8 * r : 8 * r + 8, 128 * h : 128 * h + 128] = jnp.where(left_out, MASKED, block)

    gain_w, shift_w, query_w = vecs[0:1, :], vecs[1:2, :], vecs[2:3, :]
    below64 = lax.broadcasted_iota(jnp.int32, (BOTH, 128), 1) < 64
    low_lane = lax.broadcasted_iota(jnp.int32, (BOTH, 256), 1) < D
    flats = []
    kept = []

    def send_back(p):
        per_window, normed, inverse = kept[p]
        rows = []
        for w, (prob_low, score_low, key_w) in enumerate(per_window):
            value_g = dot(prob_low, u_heads[2 * p + w])
            key_g = dot(score_low, q_heads[2 * p + w]) * SCALE
            query_all = dot_tn(score_low, key_w)
            query_g = None
            for h in range(HEADS):
                term = query_all[h * 128 : h * 128 + WTOK] * head_mask[h : h + 1, :].astype(jnp.float32)
                query_g = term if query_g is None else query_g + term
            rows.append(jnp.concatenate([low(query_g * SCALE), low(key_g), low(value_g)], 1))
        hidden_grad = dot_nt(jnp.concatenate(rows, 0), w_qkv[...])
        scaled = hidden_grad * gain_w
        mean_g = jnp.sum(scaled, 1, keepdims=True) * (1.0 / D)
        mean_gn = jnp.sum(scaled * normed, 1, keepdims=True) * (1.0 / D)
        branch = jnp.where(low_lane, inverse * (scaled - mean_g - normed * mean_gn), 0.0)
        second = branch[:, 128:256]
        stacked = jnp.concatenate([branch[:, 0:128], second, pltpu.roll(second, 64, 1)], 0)
        ret_send[p] = low(dot(ret_pack[...], low(stacked)))
        for k in range(2):
            backward(p, k, True).start()


    for p in range(2):
        for k in range(4):
            forward(p, k, False).wait_recv()
        got = [
            recv_buf[pl.ds(FWD[k][0] + p * (FWD_CUT[k % 2] - 16), FWD_CUT[k % 2]), :] for k in range(4)
        ]
        tokens = dot(take_remote[pl.ds(3 * BOTH * p, 3 * BOTH), :], jnp.concatenate(got, 0))
        x_a, x_b, x_c = tokens[0:BOTH], tokens[BOTH : 2 * BOTH], tokens[2 * BOTH :]
        tail = jnp.where(below64, x_c, 0.0)
        center = (jnp.sum(x_a, 1, keepdims=True) + jnp.sum(tail, 1, keepdims=True)) * (1.0 / D)
        c_a = x_a - center
        c_t = jnp.where(below64, x_c - center, 0.0)
        spread_sq = (
            jnp.sum(c_a * c_a, 1, keepdims=True) + jnp.sum(c_t * c_t, 1, keepdims=True)
        ) * (1.0 / D)
        inverse = lax.rsqrt(spread_sq + EPSILON)
        normed = jnp.concatenate([c_a, c_t], 1) * inverse
        hidden = low(normed * gain_w + shift_w)
        projected = dot(hidden, w_qkv[...])
        queries = low(projected[:, 0:256] + query_w)
        keys = low(projected[:, 256:512])
        values = low(projected[:, 512:768])
        incoming = low(jnp.concatenate([x_b, x_c], 1))
        upstream = low(dot_nt(incoming, w_proj[...]))

        per_window = []
        score_sum = None
        for w in range(2):
            span = slice(w * WTOK, (w + 1) * WTOK)
            q_w, u_w = q_heads.at[2 * p + w], u_heads.at[2 * p + w]
            for h in range(HEADS):
                mask = head_mask[h : h + 1, :]
                q_w[pl.ds(h * 128, WTOK), :] = queries[span] * mask
                u_w[pl.ds(h * 128, WTOK), :] = upstream[span] * mask
            scores = dot_nt(keys[span], q_w[...]) * SCALE + bias[p]
            weights = jnp.exp(scores)
            probs = weights * (1.0 / jnp.sum(weights, 0, keepdims=True))
            prob_grad = dot_nt(values[span], u_w[...])
            inner = jnp.sum(probs * prob_grad, 0, keepdims=True)
            score_grad = probs * (prob_grad - inner)
            score_sum = score_grad if score_sum is None else score_sum + score_grad
            per_window.append((low(probs), low(score_grad), keys[span]))
        kept.append((per_window, normed, inverse))

        for h in range(HEADS):
            near = far = None
            for r in range(WLON):
                s = 8 * (WLON - 1 - r)
                block = score_sum[8 * r : 8 * r + 8, 128 * h : 128 * h + 128]
                if s:
                    block = pltpu.roll(block, s, 1)
                    wrapped = jnp.where(lane8 < s, block, 0.0)
                    block = jnp.where(lane8 < s, 0.0, block)
                    far = wrapped if far is None else far + wrapped
                near = block if near is None else near + block
            fold_buf[0, 8 * h : 8 * h + 8, :] = near
            fold_buf[1, 8 * h : 8 * h + 8, :] = far
        by_row = [
            jnp.concatenate([fold_buf[part, pl.ds(b, 8, stride=8), :] for part in range(2)], 1)
            for b in range(WLAT)
        ]
        lines = dot(low(jnp.concatenate(by_row, 0)), spread[...])
        flat = None
        for b in range(WLAT):
            line = lines[8 * b : 8 * b + 8]
            if b or p:
                line = pltpu.roll(line, SPAN * b + 52 * p, 1)
            flat = line if flat is None else flat + line
        flats.append(flat)
        if p == 0:
            send_back(0)

    tiles = [flats[p][:, 128 * k : 128 * k + 128] for p in range(2) for k in range(7)]
    tiles += [jnp.zeros((8, 128), jnp.float32)] * 2
    for c in range(8):
        red_src[c] = low(jnp.concatenate(tiles[2 * c : 2 * c + 2], 0))
    reduced = []
    for s in range(1, 8):
        rank, peer = plane_peer(s)
        copy = pltpu.make_async_remote_copy(
            src_ref=red_src.at[rank],
            dst_ref=red_in.at[s - 1],
            send_sem=red_send.at[s - 1],
            recv_sem=red_recv.at[s - 1],
            device_id=peer,
            device_id_type=MESH,
        )
        copy.start()
        reduced.append(copy)

    send_back(1)
    for copy in reduced:
        copy.wait_recv()
    total = red_src[plane_me].astype(jnp.float32)
    for s in range(7):
        total = total + red_in[s].astype(jnp.float32)
    z_slots[z_me] = low(total)
    pl.semaphore_wait(ready, 2)
    along = []
    for s in range(1, 8):
        copy = pltpu.make_async_remote_copy(
            src_ref=z_slots.at[z_me],
            dst_ref=z_slots.at[z_me],
            send_sem=z_send.at[s - 1],
            recv_sem=z_recv.at[s - 1],
            device_id=z_peer(s),
            device_id_type=MESH,
        )
        copy.start()
        along.append(copy)

    for p in range(2):
        for k in range(2, 4):
            backward(p, k, True).start()

    for copy in along:
        copy.wait_recv()
    total = z_slots[0].astype(jnp.float32)
    for z in range(1, 8):
        total = total + z_slots[z].astype(jnp.float32)
    final[...] = total
    own_slot = pltpu.make_async_copy(final, all_slots.at[plane_me], out_sem.at[2])
    own_slot.start()
    gathered = []
    for s in range(1, 8):
        _, peer = plane_peer(s)
        copy = pltpu.make_async_remote_copy(
            src_ref=final,
            dst_ref=all_slots.at[plane_me],
            send_sem=all_send.at[s - 1],
            recv_sem=all_recv.at[s - 1],
            device_id=peer,
            device_id_type=MESH,
        )
        copy.start()
        gathered.append(copy)

    written = []
    for p in range(2):
        rows = pl.ds((1 - p) * TOK, TOK)
        for k in range(4):
            backward(p, k, False).wait_recv()
        got = dot(put_remote[...], ret_recv[p])
        rest = got[TOK : 2 * TOK] + pltpu.roll(got[2 * TOK :], 64, 1)
        grad_held[rows, 0:128] = low(out_grad[rows, 0:128].astype(jnp.float32) + got[0:TOK])
        grad_held[rows, 128:D] = low(out_grad[rows, 128:D].astype(jnp.float32) + rest[:, 0 : D - 128])
        copy = pltpu.make_async_copy(grad_held.at[rows], grad_out.at[rows], out_sem.at[p])
        copy.start()
        written.append(copy)

    for copy in gathered:
        copy.wait_recv()
    for copy in written + [own_slot]:
        copy.wait()
    for p in range(2):
        for k in range(4):
            forward(p, k, False).wait_send()
            backward(p, k, False).wait_send()
    for copy in reduced + along + gathered:
        copy.wait_send()


def hand_over(grad, slots, grad_out, table_out, grad_held, slots_held, table_held, sems):
    read_slots = pltpu.make_async_copy(slots, slots_held, sems.at[0, 3])
    read_slots.start()
    reads, writes = [], []
    for i in range(3):
        rows = pl.ds(96 * i, 96)
        reads.append(pltpu.make_async_copy(grad.at[rows], grad_held.at[rows], sems.at[0, i]))
        writes.append(pltpu.make_async_copy(grad_held.at[rows], grad_out.at[rows], sems.at[1, i]))
    for copy in reads:
        copy.start()
    table_held[...] = jnp.zeros((HEADS, 1, REL), jnp.float32)
    read_slots.wait()
    for tile in range(14):
        start = 128 * tile if tile < 7 else 2432 + 128 * (tile - 7)
        size = min(128, REL - start)
        for h in range(HEADS):
            entries = slots_held[tile // 2, pl.ds(8 * (tile % 2) + h, 1), :]
            table_held[h, :, start : start + size] = entries[:, 0:size]
    write_table = pltpu.make_async_copy(table_held, table_out, sems.at[1, 3])
    write_table.start()
    for read, write in zip(reads, writes):
        read.wait()
        write.start()
    for copy in writes + [write_table]:
        copy.wait()


def local(n_lon, n_lat, latent, out_grad, gain, shift, qkv_weight, query_bias, proj_weight, bias_table, band_rows):
    del band_rows
    consts = [jnp.asarray(c) for c in constants()]
    args = [
        latent.reshape(2 * TOK, D),
        out_grad.reshape(2 * TOK, D),
        gain.reshape(1, D),
        shift.reshape(1, D),
        qkv_weight,
        query_bias.reshape(1, D),
        proj_weight,
        bias_table.reshape(HEADS, 1, REL),
    ] + consts
    bf16, f32 = jnp.bfloat16, jnp.float32
    dma = pltpu.SemaphoreType.DMA
    scratch = [pltpu.VMEM(a.shape, a.dtype) for a in args] + [
        pltpu.VMEM((FWD_ROWS, 128), bf16),
        pltpu.VMEM((FWD_ROWS, 128), bf16),
        pltpu.VMEM((2, RET_ROWS, 128), bf16),
        pltpu.VMEM((2, RET_ROWS, 128), bf16),
        pltpu.VMEM((2, WTOK, LANES), f32),
        pltpu.VMEM((8, WIDE), f32),
        pltpu.VMEM((2, 64, 128), f32),
        pltpu.VMEM((8, 256), f32),
        pltpu.VMEM((256, LANES), bf16),
        pltpu.VMEM((256, 256), bf16),
        pltpu.VMEM((4, LANES, 256), bf16),
        pltpu.VMEM((4, LANES, 256), bf16),
        pltpu.VMEM((8, 16, 128), bf16),
        pltpu.VMEM((7, 16, 128), bf16),
        pltpu.VMEM((8, 16, 128), bf16),
        pltpu.VMEM((16, 128), f32),
        pltpu.VMEM((2 * TOK, D), bf16),
        dma((3,)),
        dma((len(args),)),
        dma((2, 4)),
        dma((2, 4)),
        dma((2, 4)),
        dma((2, 4)),
        dma((7,)),
        dma((7,)),
        dma((7,)),
        dma((7,)),
        dma((7,)),
        dma((7,)),
        pltpu.SemaphoreType.REGULAR,
    ]
    grad, slots = pl.pallas_call(
        functools.partial(kernel, n_lon, n_lat, len(args)),
        out_shape=(
            jax.ShapeDtypeStruct((2 * TOK, D), bf16),
            jax.ShapeDtypeStruct((8, 16, 128), f32),
        ),
        in_specs=[pl.BlockSpec(memory_space=pltpu.HBM)] * len(args),
        out_specs=(pl.BlockSpec(memory_space=pltpu.HBM), pl.BlockSpec(memory_space=pltpu.HBM)),
        scratch_shapes=scratch,
        compiler_params=pltpu.CompilerParams(
            collective_id=0, has_side_effects=True, vmem_limit_bytes=63 * 1024 * 1024
        ),
    )(*args)
    grad, table = pl.pallas_call(
        hand_over,
        out_shape=(
            jax.ShapeDtypeStruct((2 * TOK, D), bf16),
            jax.ShapeDtypeStruct((HEADS, 1, REL), f32),
        ),
        in_specs=[pl.BlockSpec(memory_space=pltpu.HBM)] * 2,
        out_specs=(pl.BlockSpec(memory_space=pltpu.HBM), pl.BlockSpec(memory_space=pltpu.HBM)),
        scratch_shapes=[
            pltpu.VMEM((2 * TOK, D), bf16),
            pltpu.VMEM((8, 16, 128), f32),
            pltpu.VMEM((HEADS, 1, REL), f32),
            dma((2, 4)),
        ],
        compiler_params=pltpu.CompilerParams(vmem_limit_bytes=63 * 1024 * 1024),
    )(grad, slots)
    return grad.reshape(latent.shape), table.reshape(bias_table.shape)


def solution(mesh):
    in_specs = (
        P(None, "lat", "lon", None),
        P(None, "lat", "lon", None),
        P(),
        P(),
        P(),
        P(),
        P(),
        P("lat", None, None, None),
        P("lat"),
    )
    out_specs = (P(None, "lat", "lon", None), P("lat", None, None, None))
    body = functools.partial(local, mesh.shape["lon"], mesh.shape["lat"])
    return jax.shard_map(body, mesh=mesh, in_specs=in_specs, out_specs=out_specs, check_vma=False)
```

```python
import functools

import jax
import jax.numpy as jnp
import ml_dtypes
import numpy as np
from jax import lax
from jax.experimental import pallas as pl
from jax.experimental.pallas import tpu as pltpu
from jax.sharding import PartitionSpec as P

HEADS = 6
D = 192
WLAT = 6
WLON = 12
ROWS = 6
COLS = 24
REL = 3312
SPAN = 2 * WLON - 1
FLAT = SPAN * WLAT * WLAT
EPSILON = 1e-05
SCALE = 32 ** (-0.5)
TOK = ROWS * COLS
WTOK = 96
BOTH = 2 * WTOK
FWD = ((0, 336), (336, 112), (448, 336), (784, 112))
FWD_ROWS = 896
FWD_WIDE = ((0, 112), (112, 64), (176, 96), (272, 64))
FWD_NARROW = (None, (0, 64), None, (64, 48))
SEEN_WIDE = ((0, 112), (96, 80), (160, 112), (256, 80))
SEEN_NARROW = (None, (0, 64), None, (48, 64))
RET = ((0, 96), (96, 32), (128, 96), (224, 32))
RET_ROWS = 256
LANES = HEADS * 128
WIDE = 896
MASKED = -1e30
MESH = pl.DeviceIdType.MESH


def constants():
    def token(row, col):
        return row * COLS + col

    def wrow(rolled_row, rolled_col):
        return (rolled_col // WLON) * WTOK + (rolled_col % WLON) * 8 + rolled_row

    groups = [
        [
            (token(r, c), wrow((r + 3) % ROWS, (c + 18) % COLS))
            for part in cols
            for r in rows
            for c in part
        ]
        for rows in (range(3, ROWS), range(3))
        for cols in ((range(6, 18), range(18, COLS)), (range(6),))
    ]

    pack = np.zeros((FWD_ROWS, 6 * TOK), np.float32)
    take_remote = np.zeros((4, 3 * WTOK, 288), np.float32)
    ret_pack = np.zeros((RET_ROWS, 3 * BOTH), np.float32)
    put_remote = np.zeros((3 * TOK, RET_ROWS), np.float32)
    for quarter, ((at, _), (back, _), group) in enumerate(zip(FWD, RET, groups)):
        n = len(group)
        for k, (t, w) in enumerate(group):
            wide = quarter % 2 == 0
            first, count, mine = (0, n, 1) if not wide else (0, 36, 0) if k < 36 else (36, 18, 1)
            for p in range(2):
                stage = 2 * p + mine
                seen_at = (SEEN_WIDE if wide else SEEN_NARROW)[stage][0]
                column = (0, 80, 144, 224)[quarter] if mine else 56 * quarter
                for part in range(3):
                    row = 3 * (p * n + first) + part * count + k - first
                    pack[at + row, (3 * p + part) * TOK + t] = 1
                    take_remote[stage, part * WTOK + w % WTOK, column + row - seen_at] = 1
            ret_pack[back + k, w] = 1
            put_remote[t, back + k] = 1
            high = k >= n // 2
            slot = back + n + k % (n // 2)
            ret_pack[slot, (2 if high else 1) * BOTH + w] = 1
            put_remote[(2 if high else 1) * TOK + t, slot] = 1
    tails = np.zeros((2, D, 128), np.float32)
    for i in range(64):
        tails[0, 128 + i, i] = 1
        tails[1, 128 + i, 64 + i] = 1
    spread = np.zeros((256, WIDE), np.float32)
    for d in range(SPAN):
        for a in range(WLAT):
            spread[8 * d + a, SPAN * WLAT * a + d] = 1
    qkv_pad = np.zeros((3 * D, LANES), np.float32)
    for part in range(3):
        for i in range(D):
            qkv_pad[part * D + i, part * 256 + i] = 1
    proj_pad = np.zeros((D, 256), np.float32)
    for i in range(D):
        proj_pad[i, i if i < 128 else 64 + i] = 1
    head_mask = np.zeros((16, 256), np.float32)
    for h in range(HEADS):
        head_mask[h, h * 32 : (h + 1) * 32] = 1
    matrices = (
        pack,
        tails.reshape(2 * D, 128),
        take_remote.reshape(12 * WTOK, 288),
        ret_pack,
        put_remote,
        spread,
        qkv_pad,
        proj_pad,
        head_mask,
    )
    return tuple(m.astype(ml_dtypes.bfloat16) for m in matrices)


def dot(a, b):
    return jnp.dot(a, b, preferred_element_type=jnp.float32)


def dot_nt(a, b):
    return lax.dot_general(a, b, (((1,), (1,)), ((), ())), preferred_element_type=jnp.float32)


def dot_tn(a, b):
    return lax.dot_general(a, b, (((0,), (0,)), ((), ())), preferred_element_type=jnp.float32)


def low(a):
    return a.astype(jnp.bfloat16)


def kernel(n_lon, n_lat, n_in, *refs):
    ins, refs = refs[:n_in], refs[n_in:]
    (grad_out, all_slots), refs = refs[:2], refs[2:]
    held, refs = refs[:n_in], refs[n_in:]
    (
        send_buf,
        recv_buf,
        ret_send,
        ret_recv,
        bias,
        table_pad,
        fold_buf,
        vecs,
        w_qkv,
        w_proj,
        q_heads,
        u_heads,
        red_src,
        red_in,
        z_slots,
        final,
        grad_held,
        out_sem,
        in_sem,
        fwd_send,
        fwd_recv,
        back_send,
        back_recv,
        red_send,
        red_recv,
        z_send,
        z_recv,
        all_send,
        all_recv,
        row_held,
        row_sem,
        ready,
    ) = refs
    (
        latent,
        out_grad,
        gain,
        shift,
        qkv_weight,
        query_bias,
        proj_weight,
        bias_table,
        pack,
        tails,
        take_remote,
        ret_pack,
        put_remote,
        spread,
        qkv_pad,
        proj_pad,
        head_mask,
    ) = held

    lon, lat = lax.axis_index("lon"), lax.axis_index("lat")
    lon_m = lax.rem(lon + n_lon - 1, n_lon)
    lat_m = lax.rem(lat + n_lat - 1, n_lat)
    two_on, two_back = lax.rem(lat + 2, n_lat), lax.rem(lat + n_lat - 2, n_lat)

    def at(lon_at, lat_at):
        return {"lon": lon_at, "lat": lat_at}

    def half_way(strip):
        return (strip // 16) * 16 + lax.rem(strip + 8, 16)

    upper = lax.rem(lat, 2)

    def lat_worker(band):
        return lax.rem(band + 2 * lax.rem(band, 2), n_lat)

    job_lat = lax.rem(lat + n_lat - 2 * upper, n_lat)
    job_lat_p = lax.rem(job_lat + 1, n_lat)
    job = half_way(lon)
    job_p = lax.rem(job + 1, n_lon)
    workers = (
        at(half_way(lon), lat_worker(lat)),
        at(half_way(lon_m), lat_worker(lat)),
        at(half_way(lon), lat_worker(lat_m)),
        at(half_way(lon_m), lat_worker(lat_m)),
    )
    homes = (at(job, job_lat), at(job_p, job_lat), at(job, job_lat_p), at(job_p, job_lat_p))
    z_me = lax.rem(lon // 2, 8)
    y_me = lon // 16
    plane_me = y_me * 2 + lax.rem(lon, 2)

    def plane_peer(step):
        rank = lax.rem(plane_me + step, 8)
        return rank, at(((rank // 2) * 8 + z_me) * 2 + lax.rem(rank, 2), lat)

    def z_peer(step):
        z = lax.rem(z_me + step, 8)
        return at((y_me * 8 + z) * 2 + lax.rem(lon, 2), lat)

    z_ring = lax.rem(lat, 2) * 8 + z_me

    def ring_peer(step):
        z = lax.rem(z_ring + step + 16, 16)
        return at((y_me * 8 + lax.rem(z, 8)) * 2 + lax.rem(lon, 2), (lat // 2) * 2 + z // 8)

    barrier = pltpu.get_barrier_semaphore()
    everyone = list(homes[2:] + homes[:2])
    everyone += [ring_peer(s) for s in range(-4, 5) if s]
    everyone += [plane_peer(s)[1] for s in range(1, 8)]
    for peer in everyone:
        pl.semaphore_signal(barrier, inc=1, device_id=peer, device_id_type=MESH)

    @pl.when(upper == 1)
    def _():
        pl.semaphore_signal(barrier, inc=1, device_id=at(lon, two_back), device_id_type=MESH)

    loads = [pltpu.make_async_copy(s, d, in_sem.at[i]) for i, (s, d) in enumerate(zip(ins, held))]
    order = [0, 1, 9, 8, 4, 14, 6, 15, 13, 7, 2, 3, 5, 16, 10, 11, 12]
    for i in order:
        loads[i].start()
    for i in (0, 1, 9, 8):
        loads[i].wait()

    source = []
    for p in range(2):
        rows = pl.ds((1 - p) * TOK, TOK)
        mixed = dot(latent[rows, :], tails[0:D, :]) + dot(out_grad[rows, :], tails[D : 2 * D, :])
        source += [latent[rows, 0:128], out_grad[rows, 0:128], low(mixed)]
    send_buf[...] = low(dot(pack[...], jnp.concatenate(source, 0)))

    pl.semaphore_wait(barrier, len(everyone) + upper)
    for step in (-4, 4):
        pl.semaphore_signal(ready, inc=1, device_id=ring_peer(step), device_id_type=MESH)
    def pick(k, places):
        here, there = places[k], places[(k + 2) % 4]
        return {name: jnp.where(upper == 0, here[name], there[name]) for name in here}

    def forward(stage, k, moved):
        q = lax.rem(k + 2 * upper, 4) if moved else k
        offset, size = (FWD_NARROW if k % 2 else FWD_WIDE)[stage]
        start = pl.multiple_of((q // 2) * FWD[2][0] + FWD[k % 2][0] + offset, 16)
        return pltpu.make_async_remote_copy(
            src_ref=send_buf.at[pl.ds(start, size)],
            dst_ref=recv_buf.at[pl.ds(start, size)],
            send_sem=fwd_send.at[stage, q],
            recv_sem=fwd_recv.at[stage, q],
            device_id=pick(k, workers) if moved else workers[k],
            device_id_type=MESH,
        )

    def backward(p, k, moved):
        q = lax.rem(k + 2 * upper, 4) if moved else k
        start = pl.multiple_of((q // 2) * RET[2][0] + RET[k % 2][0], 16)
        return pltpu.make_async_remote_copy(
            src_ref=ret_send.at[p, pl.ds(start, RET[k][1])],
            dst_ref=ret_recv.at[p, pl.ds(start, RET[k][1])],
            send_sem=back_send.at[p, q],
            recv_sem=back_recv.at[p, q],
            device_id=pick(k, homes) if moved else homes[k],
            device_id_type=MESH,
        )

    def pieces(stage, quarters):
        return [k for k in quarters if k % 2 == 0 or FWD_NARROW[stage]]

    later = (z_me >= 4) & (z_me <= 6)

    def send(stages, quarters):
        for stage in stages:
            for k in pieces(stage, quarters):
                forward(stage, k, True).start()

    send((0, 1), (0, 1))

    @pl.when(jnp.logical_not(later))
    def _():
        send((2, 3), (0, 1))

    send(range(4), (2, 3))

    for i in order:
        if i not in (0, 1, 9, 8):
            loads[i].wait()

    row_on = pltpu.make_async_remote_copy(
        src_ref=bias_table,
        dst_ref=row_held,
        send_sem=row_sem.at[0],
        recv_sem=row_sem.at[1],
        device_id=at(lon, two_on),
        device_id_type=MESH,
    )
    row_own = pltpu.make_async_copy(bias_table, row_held, row_sem.at[2])

    @pl.when(upper == 1)
    def _():
        row_on.start()

    @pl.when(upper == 0)
    def _():
        row_own.start()

    w_qkv[0:D, :] = low(dot(qkv_weight[...], qkv_pad[...]))
    w_qkv[D:256, :] = jnp.zeros((256 - D, LANES), jnp.bfloat16)
    w_proj[0:D, :] = low(dot(proj_weight[...], proj_pad[...]))
    w_proj[D:256, :] = jnp.zeros((256 - D, 256), jnp.bfloat16)
    vecs[...] = jnp.zeros((8, 256), jnp.float32)
    vecs[0:1, 0:D] = gain[...]
    vecs[1:2, 0:D] = shift[...]
    vecs[2:3, 0:D] = query_bias[...]
    for h in range(HEADS):
        pad = pl.ds(h * 128 + WTOK, 128 - WTOK)
        q_heads[:, pad, :] = jnp.zeros((4, 128 - WTOK, 256), jnp.bfloat16)
        u_heads[:, pad, :] = jnp.zeros((4, 128 - WTOK, 256), jnp.bfloat16)

    lane8 = lax.broadcasted_iota(jnp.int32, (8, 128), 1)
    row8 = lax.broadcasted_iota(jnp.int32, (8, 128), 0)
    last = (job_lat == n_lat - 1).astype(jnp.int32)
    query_half = (lax.rem(lane8, 8) >= 3).astype(jnp.int32)
    key_half = (row8 >= 3).astype(jnp.int32)
    left_out = (row8 >= WLAT).astype(jnp.int32) + last * (query_half ^ key_half) > 0

    @pl.when(upper == 1)
    def _():
        row_on.wait_recv()

    @pl.when(upper == 0)
    def _():
        row_own.wait()

    for p in range(2):
        table_pad[...] = jnp.zeros((8, WIDE), jnp.float32)
        if p == 0:
            for h in range(HEADS):
                table_pad[h : h + 1, :] = row_held[h, :, 0:WIDE]
        else:
            for h in range(HEADS):
                table_pad[h : h + 1, 0 : REL - 2432] = row_held[h, :, 2432:REL]
        entries = table_pad[...]
        for b in range(8):
            if b < WLAT:
                moved = pltpu.roll(entries, (2 * WIDE - SPAN * b - 52 * p) % WIDE, 1)
                top = low(moved)
                rest = low(moved - top.astype(jnp.float32))
                row = dot_nt(top, spread[...]) + dot_nt(rest, spread[...])
            else:
                row = jnp.zeros((8, 256), jnp.float32)
            fold_buf[0, 8 * b : 8 * b + 8, :] = row[:, 0:128]
            fold_buf[1, 8 * b : 8 * b + 8, :] = row[:, 128:256]
        for h in range(HEADS):
            near = fold_buf[0, pl.ds(h, 8, stride=8), :]
            far = fold_buf[1, pl.ds(h, 8, stride=8), :]
            for r in range(WLON):
                s = 8 * (WLON - 1 - r)
                if s:
                    block = pltpu.roll(jnp.where(lane8 >= s, near, far), 128 - s, 1)
                else:
                    block = near
                bias[p, 8 * r : 8 * r + 8, 128 * h : 128 * h + 128] = jnp.where(left_out, MASKED, block)

    @pl.when(later)
    def _():
        send((2, 3), (0, 1))

    gain_w, shift_w, query_w = vecs[0:1, :], vecs[1:2, :], vecs[2:3, :]
    below64 = lax.broadcasted_iota(jnp.int32, (WTOK, 128), 1) < 64
    low_lane = lax.broadcasted_iota(jnp.int32, (BOTH, 256), 1) < D
    flats = []
    kept = []

    def send_back(p):
        per_window = kept[p]
        rows = []
        for w, (prob_low, score_low, key_w, _, _) in enumerate(per_window):
            value_g = dot(prob_low, u_heads[2 * p + w])
            key_g = dot(score_low, q_heads[2 * p + w]) * SCALE
            query_all = dot_tn(score_low, key_w)
            query_g = None
            for h in range(HEADS):
                term = query_all[h * 128 : h * 128 + WTOK] * head_mask[h : h + 1, :].astype(jnp.float32)
                query_g = term if query_g is None else query_g + term
            rows.append(jnp.concatenate([low(query_g * SCALE), low(key_g), low(value_g)], 1))
        normed = jnp.concatenate([window[3] for window in per_window], 0)
        inverse = jnp.concatenate([window[4] for window in per_window], 0)
        hidden_grad = dot_nt(jnp.concatenate(rows, 0), w_qkv[...])
        scaled = hidden_grad * gain_w
        mean_g = jnp.sum(scaled, 1, keepdims=True) * (1.0 / D)
        mean_gn = jnp.sum(scaled * normed, 1, keepdims=True) * (1.0 / D)
        branch = jnp.where(low_lane, inverse * (scaled - mean_g - normed * mean_gn), 0.0)
        second = branch[:, 128:256]
        stacked = jnp.concatenate([branch[:, 0:128], second, pltpu.roll(second, 64, 1)], 0)
        ret_send[p] = low(dot(ret_pack[...], low(stacked)))
        for k in range(2):
            backward(p, k, True).start()


    for p in range(2):
        per_window = []
        score_sum = None
        for w in range(2):
            stage = 2 * p + w
            for k in pieces(stage, range(4)):
                forward(stage, k, False).wait_recv()
            got = []
            for k in range(4):
                seen = (SEEN_NARROW if k % 2 else SEEN_WIDE)[stage]
                if seen:
                    got.append(recv_buf[pl.ds(FWD[k][0] + seen[0], seen[1]), :])
            got = jnp.concatenate(got, 0)
            rows = pl.ds(3 * WTOK * stage, 3 * WTOK)
            tokens = dot(take_remote[rows, 0 : got.shape[0]], got)
            x_a, x_b, x_c = tokens[0:WTOK], tokens[WTOK : 2 * WTOK], tokens[2 * WTOK :]
            tail = jnp.where(below64, x_c, 0.0)
            center = (jnp.sum(x_a, 1, keepdims=True) + jnp.sum(tail, 1, keepdims=True)) * (1.0 / D)
            c_a = x_a - center
            c_t = jnp.where(below64, x_c - center, 0.0)
            spread_sq = (
                jnp.sum(c_a * c_a, 1, keepdims=True) + jnp.sum(c_t * c_t, 1, keepdims=True)
            ) * (1.0 / D)
            inverse = lax.rsqrt(spread_sq + EPSILON)
            normed = jnp.concatenate([c_a, c_t], 1) * inverse
            hidden = low(normed * gain_w + shift_w)
            projected = dot(hidden, w_qkv[...])
            queries = low(projected[:, 0:256] + query_w)
            keys = low(projected[:, 256:512])
            values = low(projected[:, 512:768])
            upstream = low(dot_nt(low(jnp.concatenate([x_b, x_c], 1)), w_proj[...]))
            q_w, u_w = q_heads.at[stage], u_heads.at[stage]
            for h in range(HEADS):
                mask = head_mask[h : h + 1, :]
                q_w[pl.ds(h * 128, WTOK), :] = queries * mask
                u_w[pl.ds(h * 128, WTOK), :] = upstream * mask
            scores = dot_nt(keys, q_w[...]) * SCALE + bias[p]
            weights = jnp.exp(scores)
            probs = weights * (1.0 / jnp.sum(weights, 0, keepdims=True))
            prob_grad = dot_nt(values, u_w[...])
            inner = jnp.sum(probs * prob_grad, 0, keepdims=True)
            score_grad = probs * (prob_grad - inner)
            score_sum = score_grad if score_sum is None else score_sum + score_grad
            per_window.append((low(probs), low(score_grad), keys, normed, inverse))
        kept.append(per_window)

        for h in range(HEADS):
            near = far = None
            for r in range(WLON):
                s = 8 * (WLON - 1 - r)
                block = score_sum[8 * r : 8 * r + 8, 128 * h : 128 * h + 128]
                if s:
                    block = pltpu.roll(block, s, 1)
                    wrapped = jnp.where(lane8 < s, block, 0.0)
                    block = jnp.where(lane8 < s, 0.0, block)
                    far = wrapped if far is None else far + wrapped
                near = block if near is None else near + block
            fold_buf[0, 8 * h : 8 * h + 8, :] = near
            fold_buf[1, 8 * h : 8 * h + 8, :] = far
        by_row = [
            jnp.concatenate([fold_buf[part, pl.ds(b, 8, stride=8), :] for part in range(2)], 1)
            for b in range(WLAT)
        ]
        lines = dot(low(jnp.concatenate(by_row, 0)), spread[...])
        flat = None
        for b in range(WLAT):
            line = lines[8 * b : 8 * b + 8]
            if b or p:
                line = pltpu.roll(line, SPAN * b + 52 * p, 1)
            flat = line if flat is None else flat + line
        flats.append(flat)
        if p == 0:
            send_back(0)

    tiles = [flats[p][:, 128 * k : 128 * k + 128] for p in range(2) for k in range(7)]
    tiles += [jnp.zeros((8, 128), jnp.float32)] * 2
    for c in range(8):
        red_src[c] = low(jnp.concatenate(tiles[2 * c : 2 * c + 2], 0))
    reduced = []
    for s in range(1, 8):
        rank, peer = plane_peer(s)
        copy = pltpu.make_async_remote_copy(
            src_ref=red_src.at[rank],
            dst_ref=red_in.at[s - 1],
            send_sem=red_send.at[s - 1],
            recv_sem=red_recv.at[s - 1],
            device_id=peer,
            device_id_type=MESH,
        )
        copy.start()
        reduced.append(copy)

    send_back(1)
    for copy in reduced:
        copy.wait_recv()
    total = red_src[plane_me].astype(jnp.float32)
    for s in range(7):
        total = total + red_in[s].astype(jnp.float32)
    z_slots[z_me] = low(total)
    pl.semaphore_wait(ready, 2)
    along = []
    for s in range(1, 8):
        copy = pltpu.make_async_remote_copy(
            src_ref=z_slots.at[z_me],
            dst_ref=z_slots.at[z_me],
            send_sem=z_send.at[s - 1],
            recv_sem=z_recv.at[s - 1],
            device_id=z_peer(s),
            device_id_type=MESH,
        )
        copy.start()
        along.append(copy)

    for p in range(2):
        for k in range(2, 4):
            backward(p, k, True).start()

    for copy in along:
        copy.wait_recv()
    total = z_slots[0].astype(jnp.float32)
    for z in range(1, 8):
        total = total + z_slots[z].astype(jnp.float32)
    final[...] = total
    own_slot = pltpu.make_async_copy(final, all_slots.at[plane_me], out_sem.at[2])
    gathered = []
    for s in range(8):
        rank = lax.rem(plane_me + s, 8)
        peer = at(((rank // 2) * 8 + z_me) * 2 + lax.rem(rank, 2), job_lat if s else two_back)
        gathered.append(
            pltpu.make_async_remote_copy(
                src_ref=final,
                dst_ref=all_slots.at[plane_me],
                send_sem=all_send.at[s],
                recv_sem=all_recv.at[s],
                device_id=peer,
                device_id_type=MESH,
            )
        )
    for copy in gathered[1:]:
        copy.start()

    @pl.when(upper == 1)
    def _():
        gathered[0].start()

    @pl.when(upper == 0)
    def _():
        own_slot.start()

    written = []
    for p in range(2):
        rows = pl.ds((1 - p) * TOK, TOK)
        for k in range(4):
            backward(p, k, False).wait_recv()
        got = dot(put_remote[...], ret_recv[p])
        rest = got[TOK : 2 * TOK] + pltpu.roll(got[2 * TOK :], 64, 1)
        grad_held[rows, 0:128] = low(out_grad[rows, 0:128].astype(jnp.float32) + got[0:TOK])
        grad_held[rows, 128:D] = low(out_grad[rows, 128:D].astype(jnp.float32) + rest[:, 0 : D - 128])
        copy = pltpu.make_async_copy(grad_held.at[rows], grad_out.at[rows], out_sem.at[p])
        copy.start()
        written.append(copy)

    for stage in range(4):
        for k in pieces(stage, range(4)):
            forward(stage, k, False).wait_send()
    for p in range(2):
        for k in range(4):
            backward(p, k, False).wait_send()
    for copy in reduced + along:
        copy.wait_send()
    for copy in written:
        copy.wait()

    @pl.when(upper == 1)
    def _():
        row_on.wait_send()
        gathered[0].wait_recv()
        gathered[0].wait_send()

    @pl.when(upper == 0)
    def _():
        own_slot.wait()

    for copy in gathered[1:]:
        copy.wait_recv()
    for copy in gathered[1:]:
        copy.wait_send()


def hand_over(grad, slots, grad_out, table_out, grad_held, slots_held, table_held, sems):
    read_slots = pltpu.make_async_copy(slots, slots_held, sems.at[0, 3])
    read_slots.start()
    reads, writes = [], []
    for i in range(3):
        rows = pl.ds(96 * i, 96)
        reads.append(pltpu.make_async_copy(grad.at[rows], grad_held.at[rows], sems.at[0, i]))
        writes.append(pltpu.make_async_copy(grad_held.at[rows], grad_out.at[rows], sems.at[1, i]))
    for copy in reads:
        copy.start()
    table_held[...] = jnp.zeros((HEADS, 1, REL), jnp.float32)
    read_slots.wait()
    for tile in range(14):
        start = 128 * tile if tile < 7 else 2432 + 128 * (tile - 7)
        size = min(128, REL - start)
        for h in range(HEADS):
            entries = slots_held[tile // 2, pl.ds(8 * (tile % 2) + h, 1), :]
            table_held[h, :, start : start + size] = entries[:, 0:size]
    write_table = pltpu.make_async_copy(table_held, table_out, sems.at[1, 3])
    write_table.start()
    for read, write in zip(reads, writes):
        read.wait()
        write.start()
    for copy in writes + [write_table]:
        copy.wait()


def local(n_lon, n_lat, latent, out_grad, gain, shift, qkv_weight, query_bias, proj_weight, bias_table, band_rows):
    del band_rows
    consts = [jnp.asarray(c) for c in constants()]
    args = [
        latent.reshape(2 * TOK, D),
        out_grad.reshape(2 * TOK, D),
        gain.reshape(1, D),
        shift.reshape(1, D),
        qkv_weight,
        query_bias.reshape(1, D),
        proj_weight,
        bias_table.reshape(HEADS, 1, REL),
    ] + consts
    bf16, f32 = jnp.bfloat16, jnp.float32
    dma = pltpu.SemaphoreType.DMA
    scratch = [pltpu.VMEM(a.shape, a.dtype) for a in args] + [
        pltpu.VMEM((FWD_ROWS, 128), bf16),
        pltpu.VMEM((FWD_ROWS, 128), bf16),
        pltpu.VMEM((2, RET_ROWS, 128), bf16),
        pltpu.VMEM((2, RET_ROWS, 128), bf16),
        pltpu.VMEM((2, WTOK, LANES), f32),
        pltpu.VMEM((8, WIDE), f32),
        pltpu.VMEM((2, 64, 128), f32),
        pltpu.VMEM((8, 256), f32),
        pltpu.VMEM((256, LANES), bf16),
        pltpu.VMEM((256, 256), bf16),
        pltpu.VMEM((4, LANES, 256), bf16),
        pltpu.VMEM((4, LANES, 256), bf16),
        pltpu.VMEM((8, 16, 128), bf16),
        pltpu.VMEM((7, 16, 128), bf16),
        pltpu.VMEM((8, 16, 128), bf16),
        pltpu.VMEM((16, 128), f32),
        pltpu.VMEM((2 * TOK, D), bf16),
        dma((3,)),
        dma((len(args),)),
        dma((4, 4)),
        dma((4, 4)),
        dma((2, 4)),
        dma((2, 4)),
        dma((7,)),
        dma((7,)),
        dma((7,)),
        dma((7,)),
        dma((8,)),
        dma((8,)),
        pltpu.VMEM((HEADS, 1, REL), f32),
        dma((3,)),
        pltpu.SemaphoreType.REGULAR,
    ]
    grad, slots = pl.pallas_call(
        functools.partial(kernel, n_lon, n_lat, len(args)),
        out_shape=(
            jax.ShapeDtypeStruct((2 * TOK, D), bf16),
            jax.ShapeDtypeStruct((8, 16, 128), f32),
        ),
        in_specs=[pl.BlockSpec(memory_space=pltpu.HBM)] * len(args),
        out_specs=(pl.BlockSpec(memory_space=pltpu.HBM), pl.BlockSpec(memory_space=pltpu.HBM)),
        scratch_shapes=scratch,
        compiler_params=pltpu.CompilerParams(
            collective_id=0, has_side_effects=True, vmem_limit_bytes=63 * 1024 * 1024
        ),
    )(*args)
    grad, table = pl.pallas_call(
        hand_over,
        out_shape=(
            jax.ShapeDtypeStruct((2 * TOK, D), bf16),
            jax.ShapeDtypeStruct((HEADS, 1, REL), f32),
        ),
        in_specs=[pl.BlockSpec(memory_space=pltpu.HBM)] * 2,
        out_specs=(pl.BlockSpec(memory_space=pltpu.HBM), pl.BlockSpec(memory_space=pltpu.HBM)),
        scratch_shapes=[
            pltpu.VMEM((2 * TOK, D), bf16),
            pltpu.VMEM((8, 16, 128), f32),
            pltpu.VMEM((HEADS, 1, REL), f32),
            dma((2, 4)),
        ],
        compiler_params=pltpu.CompilerParams(vmem_limit_bytes=63 * 1024 * 1024),
    )(grad, slots)
    return grad.reshape(latent.shape), table.reshape(bias_table.shape)


def solution(mesh):
    in_specs = (
        P(None, "lat", "lon", None),
        P(None, "lat", "lon", None),
        P(),
        P(),
        P(),
        P(),
        P(),
        P("lat", None, None, None),
        P("lat"),
    )
    out_specs = (P(None, "lat", "lon", None), P("lat", None, None, None))
    body = functools.partial(local, mesh.shape["lon"], mesh.shape["lat"])
    return jax.shard_map(body, mesh=mesh, in_specs=in_specs, out_specs=out_specs, check_vma=False)
```

```python
import functools

import jax
import jax.numpy as jnp
import ml_dtypes
import numpy as np
from jax import lax
from jax.experimental import pallas as pl
from jax.experimental.pallas import tpu as pltpu
from jax.sharding import PartitionSpec as P

HEADS = 6
D = 192
WLAT = 6
WLON = 12
ROWS = 6
COLS = 24
REL = 3312
SPAN = 2 * WLON - 1
FLAT = SPAN * WLAT * WLAT
EPSILON = 1e-05
SCALE = 32 ** (-0.5)
TOK = ROWS * COLS
WTOK = 96
BOTH = 2 * WTOK
FWD = ((0, 336), (336, 112), (448, 336), (784, 112))
FWD_ROWS = 896
FWD_WIDE = ((0, 112), (112, 64), (176, 96), (272, 64))
FWD_NARROW = (None, (0, 64), None, (64, 48))
SEEN_WIDE = ((0, 112), (96, 80), (160, 112), (256, 80))
SEEN_NARROW = (None, (0, 64), None, (48, 64))
RET = ((0, 96), (96, 32), (128, 96), (224, 32))
RET_ROWS = 256
LANES = HEADS * 128
WIDE = 896
MASKED = -1e30
FAR_FIRST = (4, 3, 5, 2, 6, 7, 1)
MESH = pl.DeviceIdType.MESH


def constants():
    def token(row, col):
        return row * COLS + col

    def wrow(rolled_row, rolled_col):
        return (rolled_col // WLON) * WTOK + (rolled_col % WLON) * 8 + rolled_row

    groups = [
        [
            (token(r, c), wrow((r + 3) % ROWS, (c + 18) % COLS))
            for part in cols
            for r in rows
            for c in part
        ]
        for rows in (range(3, ROWS), range(3))
        for cols in ((range(6, 18), range(18, COLS)), (range(6),))
    ]

    pack = np.zeros((FWD_ROWS, 6 * TOK), np.float32)
    take_remote = np.zeros((4, 3 * WTOK, 288), np.float32)
    ret_pack = np.zeros((RET_ROWS, 3 * BOTH), np.float32)
    put_remote = np.zeros((3 * TOK, RET_ROWS), np.float32)
    for quarter, ((at, _), (back, _), group) in enumerate(zip(FWD, RET, groups)):
        n = len(group)
        for k, (t, w) in enumerate(group):
            wide = quarter % 2 == 0
            first, count, mine = (0, n, 1) if not wide else (0, 36, 0) if k < 36 else (36, 18, 1)
            for p in range(2):
                stage = 2 * p + mine
                seen_at = (SEEN_WIDE if wide else SEEN_NARROW)[stage][0]
                column = (0, 80, 144, 224)[quarter] if mine else 56 * quarter
                for part in range(3):
                    row = 3 * (p * n + first) + part * count + k - first
                    pack[at + row, (3 * p + part) * TOK + t] = 1
                    take_remote[stage, part * WTOK + w % WTOK, column + row - seen_at] = 1
            ret_pack[back + k, w] = 1
            put_remote[t, back + k] = 1
            high = k >= n // 2
            slot = back + n + k % (n // 2)
            ret_pack[slot, (2 if high else 1) * BOTH + w] = 1
            put_remote[(2 if high else 1) * TOK + t, slot] = 1
    tails = np.zeros((2, D, 128), np.float32)
    for i in range(64):
        tails[0, 128 + i, i] = 1
        tails[1, 128 + i, 64 + i] = 1
    spread = np.zeros((256, WIDE), np.float32)
    for d in range(SPAN):
        for a in range(WLAT):
            spread[8 * d + a, SPAN * WLAT * a + d] = 1
    qkv_pad = np.zeros((3 * D, LANES), np.float32)
    for part in range(3):
        for i in range(D):
            qkv_pad[part * D + i, part * 256 + i] = 1
    proj_pad = np.zeros((D, 256), np.float32)
    for i in range(D):
        proj_pad[i, i if i < 128 else 64 + i] = 1
    head_mask = np.zeros((16, 256), np.float32)
    for h in range(HEADS):
        head_mask[h, h * 32 : (h + 1) * 32] = 1
    matrices = (
        pack,
        tails.reshape(2 * D, 128),
        take_remote.reshape(12 * WTOK, 288),
        ret_pack,
        put_remote,
        spread,
        qkv_pad,
        proj_pad,
        head_mask,
    )
    return tuple(m.astype(ml_dtypes.bfloat16) for m in matrices)


def dot(a, b):
    return jnp.dot(a, b, preferred_element_type=jnp.float32)


def dot_nt(a, b):
    return lax.dot_general(a, b, (((1,), (1,)), ((), ())), preferred_element_type=jnp.float32)


def dot_tn(a, b):
    return lax.dot_general(a, b, (((0,), (0,)), ((), ())), preferred_element_type=jnp.float32)


def low(a):
    return a.astype(jnp.bfloat16)


def kernel(n_lon, n_lat, n_in, *refs):
    ins, refs = refs[:n_in], refs[n_in:]
    (grad_out, all_slots), refs = refs[:2], refs[2:]
    held, refs = refs[:n_in], refs[n_in:]
    (
        send_buf,
        recv_buf,
        ret_send,
        ret_recv,
        bias,
        table_pad,
        fold_buf,
        vecs,
        w_qkv,
        w_proj,
        q_heads,
        u_heads,
        red_src,
        red_in,
        z_slots,
        final,
        grad_held,
        out_sem,
        in_sem,
        fwd_send,
        fwd_recv,
        back_send,
        back_recv,
        red_send,
        red_recv,
        z_send,
        z_recv,
        all_send,
        all_recv,
        row_held,
        row_sem,
        ready,
    ) = refs
    (
        latent,
        out_grad,
        gain,
        shift,
        qkv_weight,
        query_bias,
        proj_weight,
        bias_table,
        pack,
        tails,
        take_remote,
        ret_pack,
        put_remote,
        spread,
        qkv_pad,
        proj_pad,
        head_mask,
    ) = held

    lon, lat = lax.axis_index("lon"), lax.axis_index("lat")
    lon_m = lax.rem(lon + n_lon - 1, n_lon)
    lat_m = lax.rem(lat + n_lat - 1, n_lat)
    two_on, two_back = lax.rem(lat + 2, n_lat), lax.rem(lat + n_lat - 2, n_lat)

    def at(lon_at, lat_at):
        return {"lon": lon_at, "lat": lat_at}

    def half_way(strip):
        return (strip // 16) * 16 + lax.rem(strip + 8, 16)

    upper = lax.rem(lat, 2)

    def lat_worker(band):
        return lax.rem(band + 2 * lax.rem(band, 2), n_lat)

    job_lat = lax.rem(lat + n_lat - 2 * upper, n_lat)
    job_lat_p = lax.rem(job_lat + 1, n_lat)
    job = half_way(lon)
    job_p = lax.rem(job + 1, n_lon)
    workers = (
        at(half_way(lon), lat_worker(lat)),
        at(half_way(lon_m), lat_worker(lat)),
        at(half_way(lon), lat_worker(lat_m)),
        at(half_way(lon_m), lat_worker(lat_m)),
    )
    homes = (at(job, job_lat), at(job_p, job_lat), at(job, job_lat_p), at(job_p, job_lat_p))
    z_me = lax.rem(lon // 2, 8)
    y_me = lon // 16
    plane_me = y_me * 2 + lax.rem(lon, 2)

    def plane_peer(step):
        rank = lax.rem(plane_me + step, 8)
        return rank, at(((rank // 2) * 8 + z_me) * 2 + lax.rem(rank, 2), lat)

    def z_peer(step):
        z = lax.rem(z_me + step, 8)
        return at((y_me * 8 + z) * 2 + lax.rem(lon, 2), lat)

    z_ring = lax.rem(lat, 2) * 8 + z_me

    def ring_peer(step):
        z = lax.rem(z_ring + step + 16, 16)
        return at((y_me * 8 + lax.rem(z, 8)) * 2 + lax.rem(lon, 2), (lat // 2) * 2 + z // 8)

    barrier = pltpu.get_barrier_semaphore()
    everyone = list(homes[2:] + homes[:2])
    everyone += [ring_peer(s) for s in range(-4, 5) if s]
    everyone += [plane_peer(s)[1] for s in range(1, 8)]
    for peer in everyone:
        pl.semaphore_signal(barrier, inc=1, device_id=peer, device_id_type=MESH)

    @pl.when(upper == 1)
    def _():
        pl.semaphore_signal(barrier, inc=1, device_id=at(lon, two_back), device_id_type=MESH)

    loads = [pltpu.make_async_copy(s, d, in_sem.at[i]) for i, (s, d) in enumerate(zip(ins, held))]
    order = [0, 1, 9, 8, 4, 14, 6, 15, 13, 7, 2, 3, 5, 16, 10, 11, 12]
    for i in order:
        loads[i].start()
    for i in (0, 1, 9, 8):
        loads[i].wait()

    source = []
    for p in range(2):
        rows = pl.ds((1 - p) * TOK, TOK)
        mixed = dot(latent[rows, :], tails[0:D, :]) + dot(out_grad[rows, :], tails[D : 2 * D, :])
        source += [latent[rows, 0:128], out_grad[rows, 0:128], low(mixed)]
    send_buf[...] = low(dot(pack[...], jnp.concatenate(source, 0)))

    pl.semaphore_wait(barrier, len(everyone) + upper)
    for step in (-4, 4):
        pl.semaphore_signal(ready, inc=1, device_id=ring_peer(step), device_id_type=MESH)
    def pick(k, places):
        here, there = places[k], places[(k + 2) % 4]
        return {name: jnp.where(upper == 0, here[name], there[name]) for name in here}

    def forward(stage, k, moved):
        q = lax.rem(k + 2 * upper, 4) if moved else k
        offset, size = (FWD_NARROW if k % 2 else FWD_WIDE)[stage]
        start = pl.multiple_of((q // 2) * FWD[2][0] + FWD[k % 2][0] + offset, 16)
        return pltpu.make_async_remote_copy(
            src_ref=send_buf.at[pl.ds(start, size)],
            dst_ref=recv_buf.at[pl.ds(start, size)],
            send_sem=fwd_send.at[stage, q],
            recv_sem=fwd_recv.at[stage, q],
            device_id=pick(k, workers) if moved else workers[k],
            device_id_type=MESH,
        )

    def backward(p, k, moved):
        q = lax.rem(k + 2 * upper, 4) if moved else k
        start = pl.multiple_of((q // 2) * RET[2][0] + RET[k % 2][0], 16)
        return pltpu.make_async_remote_copy(
            src_ref=ret_send.at[p, pl.ds(start, RET[k][1])],
            dst_ref=ret_recv.at[p, pl.ds(start, RET[k][1])],
            send_sem=back_send.at[p, q],
            recv_sem=back_recv.at[p, q],
            device_id=pick(k, homes) if moved else homes[k],
            device_id_type=MESH,
        )

    def pieces(stage, quarters):
        return [k for k in quarters if k % 2 == 0 or FWD_NARROW[stage]]

    later = (z_me >= 4) & (z_me <= 6)

    def send(stages, quarters):
        for stage in stages:
            for k in pieces(stage, quarters):
                forward(stage, k, True).start()

    send((0, 1), (0, 1))

    @pl.when(jnp.logical_not(later))
    def _():
        send((2, 3), (0, 1))

    send(range(4), (2, 3))

    for i in order:
        if i not in (0, 1, 9, 8):
            loads[i].wait()

    row_on = pltpu.make_async_remote_copy(
        src_ref=bias_table,
        dst_ref=row_held,
        send_sem=row_sem.at[0],
        recv_sem=row_sem.at[1],
        device_id=at(lon, two_on),
        device_id_type=MESH,
    )
    row_own = pltpu.make_async_copy(bias_table, row_held, row_sem.at[2])

    @pl.when(upper == 1)
    def _():
        row_on.start()

    @pl.when(upper == 0)
    def _():
        row_own.start()

    w_qkv[0:D, :] = low(dot(qkv_weight[...], qkv_pad[...]))
    w_qkv[D:256, :] = jnp.zeros((256 - D, LANES), jnp.bfloat16)
    w_proj[0:D, :] = low(dot(proj_weight[...], proj_pad[...]))
    w_proj[D:256, :] = jnp.zeros((256 - D, 256), jnp.bfloat16)
    vecs[...] = jnp.zeros((8, 256), jnp.float32)
    vecs[0:1, 0:D] = gain[...]
    vecs[1:2, 0:D] = shift[...]
    vecs[2:3, 0:D] = query_bias[...]
    for h in range(HEADS):
        pad = pl.ds(h * 128 + WTOK, 128 - WTOK)
        q_heads[:, pad, :] = jnp.zeros((4, 128 - WTOK, 256), jnp.bfloat16)
        u_heads[:, pad, :] = jnp.zeros((4, 128 - WTOK, 256), jnp.bfloat16)

    lane8 = lax.broadcasted_iota(jnp.int32, (8, 128), 1)
    row8 = lax.broadcasted_iota(jnp.int32, (8, 128), 0)
    last = (job_lat == n_lat - 1).astype(jnp.int32)
    query_half = (lax.rem(lane8, 8) >= 3).astype(jnp.int32)
    key_half = (row8 >= 3).astype(jnp.int32)
    left_out = (row8 >= WLAT).astype(jnp.int32) + last * (query_half ^ key_half) > 0

    @pl.when(upper == 1)
    def _():
        row_on.wait_recv()

    @pl.when(upper == 0)
    def _():
        row_own.wait()

    for p in range(2):
        table_pad[...] = jnp.zeros((8, WIDE), jnp.float32)
        if p == 0:
            for h in range(HEADS):
                table_pad[h : h + 1, :] = row_held[h, :, 0:WIDE]
        else:
            for h in range(HEADS):
                table_pad[h : h + 1, 0 : REL - 2432] = row_held[h, :, 2432:REL]
        entries = table_pad[...]
        for b in range(8):
            if b < WLAT:
                moved = pltpu.roll(entries, (2 * WIDE - SPAN * b - 52 * p) % WIDE, 1)
                top = low(moved)
                rest = low(moved - top.astype(jnp.float32))
                row = dot_nt(top, spread[...]) + dot_nt(rest, spread[...])
            else:
                row = jnp.zeros((8, 256), jnp.float32)
            fold_buf[0, 8 * b : 8 * b + 8, :] = row[:, 0:128]
            fold_buf[1, 8 * b : 8 * b + 8, :] = row[:, 128:256]
        for h in range(HEADS):
            near = fold_buf[0, pl.ds(h, 8, stride=8), :]
            far = fold_buf[1, pl.ds(h, 8, stride=8), :]
            for r in range(WLON):
                s = 8 * (WLON - 1 - r)
                if s:
                    block = pltpu.roll(jnp.where(lane8 >= s, near, far), 128 - s, 1)
                else:
                    block = near
                bias[p, 8 * r : 8 * r + 8, 128 * h : 128 * h + 128] = jnp.where(left_out, MASKED, block)

    @pl.when(later)
    def _():
        send((2, 3), (0, 1))

    gain_w, shift_w, query_w = vecs[0:1, :], vecs[1:2, :], vecs[2:3, :]
    below64 = lax.broadcasted_iota(jnp.int32, (WTOK, 128), 1) < 64
    low_lane = lax.broadcasted_iota(jnp.int32, (BOTH, 256), 1) < D
    flats = []
    kept = []

    def send_back(p):
        per_window = kept[p]
        rows = []
        for w, (prob_low, score_low, key_w, _, _) in enumerate(per_window):
            value_g = dot(prob_low, u_heads[2 * p + w])
            key_g = dot(score_low, q_heads[2 * p + w]) * SCALE
            query_all = dot_tn(score_low, key_w)
            query_g = None
            for h in range(HEADS):
                term = query_all[h * 128 : h * 128 + WTOK] * head_mask[h : h + 1, :].astype(jnp.float32)
                query_g = term if query_g is None else query_g + term
            rows.append(jnp.concatenate([low(query_g * SCALE), low(key_g), low(value_g)], 1))
        normed = jnp.concatenate([window[3] for window in per_window], 0)
        inverse = jnp.concatenate([window[4] for window in per_window], 0)
        hidden_grad = dot_nt(jnp.concatenate(rows, 0), w_qkv[...])
        scaled = hidden_grad * gain_w
        mean_g = jnp.sum(scaled, 1, keepdims=True) * (1.0 / D)
        mean_gn = jnp.sum(scaled * normed, 1, keepdims=True) * (1.0 / D)
        branch = jnp.where(low_lane, inverse * (scaled - mean_g - normed * mean_gn), 0.0)
        second = branch[:, 128:256]
        stacked = jnp.concatenate([branch[:, 0:128], second, pltpu.roll(second, 64, 1)], 0)
        ret_send[p] = low(dot(ret_pack[...], low(stacked)))
        for k in range(2):
            backward(p, k, True).start()


    for p in range(2):
        per_window = []
        score_sum = None
        for w in range(2):
            stage = 2 * p + w
            for k in pieces(stage, range(4)):
                forward(stage, k, False).wait_recv()
            got = []
            for k in range(4):
                seen = (SEEN_NARROW if k % 2 else SEEN_WIDE)[stage]
                if seen:
                    got.append(recv_buf[pl.ds(FWD[k][0] + seen[0], seen[1]), :])
            got = jnp.concatenate(got, 0)
            rows = pl.ds(3 * WTOK * stage, 3 * WTOK)
            tokens = dot(take_remote[rows, 0 : got.shape[0]], got)
            x_a, x_b, x_c = tokens[0:WTOK], tokens[WTOK : 2 * WTOK], tokens[2 * WTOK :]
            tail = jnp.where(below64, x_c, 0.0)
            center = (jnp.sum(x_a, 1, keepdims=True) + jnp.sum(tail, 1, keepdims=True)) * (1.0 / D)
            c_a = x_a - center
            c_t = jnp.where(below64, x_c - center, 0.0)
            spread_sq = (
                jnp.sum(c_a * c_a, 1, keepdims=True) + jnp.sum(c_t * c_t, 1, keepdims=True)
            ) * (1.0 / D)
            inverse = lax.rsqrt(spread_sq + EPSILON)
            normed = jnp.concatenate([c_a, c_t], 1) * inverse
            hidden = low(normed * gain_w + shift_w)
            projected = dot(hidden, w_qkv[...])
            queries = low(projected[:, 0:256] + query_w)
            keys = low(projected[:, 256:512])
            values = low(projected[:, 512:768])
            upstream = low(dot_nt(low(jnp.concatenate([x_b, x_c], 1)), w_proj[...]))
            q_w, u_w = q_heads.at[stage], u_heads.at[stage]
            for h in range(HEADS):
                mask = head_mask[h : h + 1, :]
                q_w[pl.ds(h * 128, WTOK), :] = queries * mask
                u_w[pl.ds(h * 128, WTOK), :] = upstream * mask
            scores = dot_nt(keys, q_w[...]) * SCALE + bias[p]
            weights = jnp.exp(scores)
            probs = weights * (1.0 / jnp.sum(weights, 0, keepdims=True))
            prob_grad = dot_nt(values, u_w[...])
            inner = jnp.sum(probs * prob_grad, 0, keepdims=True)
            score_grad = probs * (prob_grad - inner)
            score_sum = score_grad if score_sum is None else score_sum + score_grad
            per_window.append((low(probs), low(score_grad), keys, normed, inverse))
        kept.append(per_window)

        for h in range(HEADS):
            near = far = None
            for r in range(WLON):
                s = 8 * (WLON - 1 - r)
                block = score_sum[8 * r : 8 * r + 8, 128 * h : 128 * h + 128]
                if s:
                    block = pltpu.roll(block, s, 1)
                    wrapped = jnp.where(lane8 < s, block, 0.0)
                    block = jnp.where(lane8 < s, 0.0, block)
                    far = wrapped if far is None else far + wrapped
                near = block if near is None else near + block
            fold_buf[0, 8 * h : 8 * h + 8, :] = near
            fold_buf[1, 8 * h : 8 * h + 8, :] = far
        by_row = [
            jnp.concatenate([fold_buf[part, pl.ds(b, 8, stride=8), :] for part in range(2)], 1)
            for b in range(WLAT)
        ]
        lines = dot(low(jnp.concatenate(by_row, 0)), spread[...])
        flat = None
        for b in range(WLAT):
            line = lines[8 * b : 8 * b + 8]
            if b or p:
                line = pltpu.roll(line, SPAN * b + 52 * p, 1)
            flat = line if flat is None else flat + line
        flats.append(flat)
        if p == 0:
            send_back(0)

    tiles = [flats[p][:, 128 * k : 128 * k + 128] for p in range(2) for k in range(7)]
    tiles += [jnp.zeros((8, 128), jnp.float32)] * 2
    for c in range(8):
        red_src[c] = low(jnp.concatenate(tiles[2 * c : 2 * c + 2], 0))
    reduced = []
    for s in FAR_FIRST:
        rank, peer = plane_peer(s)
        copy = pltpu.make_async_remote_copy(
            src_ref=red_src.at[rank],
            dst_ref=red_in.at[s - 1],
            send_sem=red_send.at[s - 1],
            recv_sem=red_recv.at[s - 1],
            device_id=peer,
            device_id_type=MESH,
        )
        copy.start()
        reduced.append(copy)

    send_back(1)
    for copy in reduced:
        copy.wait_recv()
    total = red_src[plane_me].astype(jnp.float32)
    for s in range(7):
        total = total + red_in[s].astype(jnp.float32)
    z_slots[z_me] = low(total)
    pl.semaphore_wait(ready, 2)
    along = []
    for s in range(1, 8):
        copy = pltpu.make_async_remote_copy(
            src_ref=z_slots.at[z_me],
            dst_ref=z_slots.at[z_me],
            send_sem=z_send.at[s - 1],
            recv_sem=z_recv.at[s - 1],
            device_id=z_peer(s),
            device_id_type=MESH,
        )
        copy.start()
        along.append(copy)

    for p in range(2):
        for k in range(2, 4):
            backward(p, k, True).start()

    for copy in along:
        copy.wait_recv()
    total = z_slots[0].astype(jnp.float32)
    for z in range(1, 8):
        total = total + z_slots[z].astype(jnp.float32)
    final[...] = total
    own_slot = pltpu.make_async_copy(final, all_slots.at[plane_me], out_sem.at[2])
    gathered = []
    for s in range(8):
        rank = lax.rem(plane_me + s, 8)
        peer = at(((rank // 2) * 8 + z_me) * 2 + lax.rem(rank, 2), job_lat if s else two_back)
        gathered.append(
            pltpu.make_async_remote_copy(
                src_ref=final,
                dst_ref=all_slots.at[plane_me],
                send_sem=all_send.at[s],
                recv_sem=all_recv.at[s],
                device_id=peer,
                device_id_type=MESH,
            )
        )
    for s in FAR_FIRST:
        gathered[s].start()

    @pl.when(upper == 1)
    def _():
        gathered[0].start()

    @pl.when(upper == 0)
    def _():
        own_slot.start()

    written = []
    for p in range(2):
        rows = pl.ds((1 - p) * TOK, TOK)
        for k in range(4):
            backward(p, k, False).wait_recv()
        got = dot(put_remote[...], ret_recv[p])
        rest = got[TOK : 2 * TOK] + pltpu.roll(got[2 * TOK :], 64, 1)
        grad_held[rows, 0:128] = low(out_grad[rows, 0:128].astype(jnp.float32) + got[0:TOK])
        grad_held[rows, 128:D] = low(out_grad[rows, 128:D].astype(jnp.float32) + rest[:, 0 : D - 128])
        copy = pltpu.make_async_copy(grad_held.at[rows], grad_out.at[rows], out_sem.at[p])
        copy.start()
        written.append(copy)

    for stage in range(4):
        for k in pieces(stage, range(4)):
            forward(stage, k, False).wait_send()
    for p in range(2):
        for k in range(4):
            backward(p, k, False).wait_send()
    for copy in reduced + along:
        copy.wait_send()
    for copy in written:
        copy.wait()

    @pl.when(upper == 1)
    def _():
        row_on.wait_send()
        gathered[0].wait_recv()
        gathered[0].wait_send()

    @pl.when(upper == 0)
    def _():
        own_slot.wait()

    for copy in gathered[1:]:
        copy.wait_recv()
    for copy in gathered[1:]:
        copy.wait_send()


def hand_over(grad, slots, grad_out, table_out, grad_held, slots_held, table_held, sems):
    read_slots = pltpu.make_async_copy(slots, slots_held, sems.at[0, 3])
    read_slots.start()
    reads, writes = [], []
    for i in range(3):
        rows = pl.ds(96 * i, 96)
        reads.append(pltpu.make_async_copy(grad.at[rows], grad_held.at[rows], sems.at[0, i]))
        writes.append(pltpu.make_async_copy(grad_held.at[rows], grad_out.at[rows], sems.at[1, i]))
    for copy in reads:
        copy.start()
    table_held[...] = jnp.zeros((HEADS, 1, REL), jnp.float32)
    read_slots.wait()
    for tile in range(14):
        start = 128 * tile if tile < 7 else 2432 + 128 * (tile - 7)
        size = min(128, REL - start)
        for h in range(HEADS):
            entries = slots_held[tile // 2, pl.ds(8 * (tile % 2) + h, 1), :]
            table_held[h, :, start : start + size] = entries[:, 0:size]
    write_table = pltpu.make_async_copy(table_held, table_out, sems.at[1, 3])
    write_table.start()
    for read, write in zip(reads, writes):
        read.wait()
        write.start()
    for copy in writes + [write_table]:
        copy.wait()


def local(n_lon, n_lat, latent, out_grad, gain, shift, qkv_weight, query_bias, proj_weight, bias_table, band_rows):
    del band_rows
    consts = [jnp.asarray(c) for c in constants()]
    args = [
        latent.reshape(2 * TOK, D),
        out_grad.reshape(2 * TOK, D),
        gain.reshape(1, D),
        shift.reshape(1, D),
        qkv_weight,
        query_bias.reshape(1, D),
        proj_weight,
        bias_table.reshape(HEADS, 1, REL),
    ] + consts
    bf16, f32 = jnp.bfloat16, jnp.float32
    dma = pltpu.SemaphoreType.DMA
    scratch = [pltpu.VMEM(a.shape, a.dtype) for a in args] + [
        pltpu.VMEM((FWD_ROWS, 128), bf16),
        pltpu.VMEM((FWD_ROWS, 128), bf16),
        pltpu.VMEM((2, RET_ROWS, 128), bf16),
        pltpu.VMEM((2, RET_ROWS, 128), bf16),
        pltpu.VMEM((2, WTOK, LANES), f32),
        pltpu.VMEM((8, WIDE), f32),
        pltpu.VMEM((2, 64, 128), f32),
        pltpu.VMEM((8, 256), f32),
        pltpu.VMEM((256, LANES), bf16),
        pltpu.VMEM((256, 256), bf16),
        pltpu.VMEM((4, LANES, 256), bf16),
        pltpu.VMEM((4, LANES, 256), bf16),
        pltpu.VMEM((8, 16, 128), bf16),
        pltpu.VMEM((7, 16, 128), bf16),
        pltpu.VMEM((8, 16, 128), bf16),
        pltpu.VMEM((16, 128), f32),
        pltpu.VMEM((2 * TOK, D), bf16),
        dma((3,)),
        dma((len(args),)),
        dma((4, 4)),
        dma((4, 4)),
        dma((2, 4)),
        dma((2, 4)),
        dma((7,)),
        dma((7,)),
        dma((7,)),
        dma((7,)),
        dma((8,)),
        dma((8,)),
        pltpu.VMEM((HEADS, 1, REL), f32),
        dma((3,)),
        pltpu.SemaphoreType.REGULAR,
    ]
    grad, slots = pl.pallas_call(
        functools.partial(kernel, n_lon, n_lat, len(args)),
        out_shape=(
            jax.ShapeDtypeStruct((2 * TOK, D), bf16),
            jax.ShapeDtypeStruct((8, 16, 128), f32),
        ),
        in_specs=[pl.BlockSpec(memory_space=pltpu.HBM)] * len(args),
        out_specs=(pl.BlockSpec(memory_space=pltpu.HBM), pl.BlockSpec(memory_space=pltpu.HBM)),
        scratch_shapes=scratch,
        compiler_params=pltpu.CompilerParams(
            collective_id=0, has_side_effects=True, vmem_limit_bytes=63 * 1024 * 1024
        ),
    )(*args)
    grad, table = pl.pallas_call(
        hand_over,
        out_shape=(
            jax.ShapeDtypeStruct((2 * TOK, D), bf16),
            jax.ShapeDtypeStruct((HEADS, 1, REL), f32),
        ),
        in_specs=[pl.BlockSpec(memory_space=pltpu.HBM)] * 2,
        out_specs=(pl.BlockSpec(memory_space=pltpu.HBM), pl.BlockSpec(memory_space=pltpu.HBM)),
        scratch_shapes=[
            pltpu.VMEM((2 * TOK, D), bf16),
            pltpu.VMEM((8, 16, 128), f32),
            pltpu.VMEM((HEADS, 1, REL), f32),
            dma((2, 4)),
        ],
        compiler_params=pltpu.CompilerParams(vmem_limit_bytes=63 * 1024 * 1024),
    )(grad, slots)
    return grad.reshape(latent.shape), table.reshape(bias_table.shape)


def solution(mesh):
    in_specs = (
        P(None, "lat", "lon", None),
        P(None, "lat", "lon", None),
        P(),
        P(),
        P(),
        P(),
        P(),
        P("lat", None, None, None),
        P("lat"),
    )
    out_specs = (P(None, "lat", "lon", None), P("lat", None, None, None))
    body = functools.partial(local, mesh.shape["lon"], mesh.shape["lat"])
    return jax.shard_map(body, mesh=mesh, in_specs=in_specs, out_specs=out_specs, check_vma=False)
```
